512 devices in a mesh: tm: 32 (over x, z_hi, core), height: 16 (over z_lo, y).
Axes of the slice: x: 4, y: 8, z: 8 (z_hi: 4, z_lo: 2; z = z_hi * 2 + z_lo), core: 2. Of those that a mesh axis runs over, the one named last changes fastest.
Arguments:
- queries: bfloat16 [192, 128, 3, 1536], P('tm', 'height'), may hold values from -8 to 8
- keys: bfloat16 [192, 128, 3, 1536], P('tm', 'height'), may hold values from -8 to 8
- values: bfloat16 [192, 128, 3, 1536], P('tm', 'height'), may hold values from -6 to 6
- grad_out: bfloat16 [192, 128, 3, 1536], P('tm', 'height'), may hold values from -6 to 6
- window_radius: int32 [12, 2], replicated, may hold values from 0 to 1, as said below
- frames_valid: int32 [32], P('tm'), may hold values from 1 to 6, as said below
- rows_valid: int32 [16], P('height'), may hold values from 1 to 8, as said below
Outputs:
- grad_queries: bfloat16 [192, 128, 3, 1536], P('tm', 'height')
- grad_keys: bfloat16 [192, 128, 3, 1536], P('tm', 'height')
- grad_values: bfloat16 [192, 128, 3, 1536], P('tm', 'height')
The draws below stay inside these ranges and needn't reach their ends.
Inputs may be any that keep to these rules, and one draw needn't show every extreme that they name: `window_radius`: some head reaches one tile along both frames and rows. `frames_valid`: some time tile has all 6 frames valid. `rows_valid`: some height tile has all 8 rows valid.
All inputs are finite; a program needn't handle non-finite values.
Results may differ from the reference program's by a relative error of at most 0.025.
Values may be sent and summed in bfloat16 or wider, within the bound.
A program may use at most 128 MiB of HBM per device.

```python
import jax
import jax.numpy as jnp
from jax import lax

HEADS = 12
HD = 128
D = 1536
TF = 6
TR = 8
COLS = 3
CLIP_TT = 32
CLIP_HT = 16
NF = 192
NR = 128


def draw_queries(key, part):
    key = jax.random.fold_in(key, 1)
    drawn_values = jax.random.normal(jax.random.fold_in(key, 2), (NF, NR, COLS, D))
    drawn_values = jnp.clip(drawn_values, -8.0, 8.0)
    return drawn_values.astype(jnp.bfloat16)


def draw_keys(key, part):
    key = jax.random.fold_in(key, 4)
    drawn_values = jax.random.normal(jax.random.fold_in(key, 5), (NF, NR, COLS, D))
    drawn_values = jnp.clip(drawn_values, -8.0, 8.0)
    return drawn_values.astype(jnp.bfloat16)


def draw_window_radius(key, part):
    key = jax.random.fold_in(key, 7)
    radius = jax.random.randint(jax.random.fold_in(key, 1), (HEADS, 2), 0, 2)
    widest = jax.random.randint(jax.random.fold_in(key, 2), (), 0, HEADS)
    return jnp.where(jnp.arange(HEADS)[:, None] == widest, 1, radius).astype(jnp.int32)


def draw_frames_valid(key, part):
    key = jax.random.fold_in(key, 8)
    counts = jax.random.randint(jax.random.fold_in(key, 1), (NF // TF,), 1, TF + 1)
    fullest = jax.random.randint(jax.random.fold_in(key, 2), (), 0, NF // TF)
    return jnp.where(jnp.arange(NF // TF) == fullest, TF, counts).astype(jnp.int32)


def draw_rows_valid(key, part):
    key = jax.random.fold_in(key, 9)
    counts = jax.random.randint(jax.random.fold_in(key, 1), (NR // TR,), 1, TR + 1)
    fullest = jax.random.randint(jax.random.fold_in(key, 2), (), 0, NR // TR)
    return jnp.where(jnp.arange(NR // TR) == fullest, TR, counts).astype(jnp.int32)


def shard_levels(rng, shape, pieces, least, top_value):
    def one(dim, blocks):
        steps = jax.random.uniform(jax.random.fold_in(jax.random.fold_in(rng, 6), dim), (blocks,), jnp.float32, least / len(pieces), top_value / len(pieces))
        return jnp.repeat(jnp.exp(steps), shape[dim] // blocks).reshape((-1,) + (1,) * (len(shape) - dim - 1))

    gain = one(*pieces[0])
    for cut in pieces[1:]:
        gain = gain * one(*cut)
    return gain


def scatter_about(own_key, shape, deviation, bound, shards=(), kind=jnp.bfloat16):
    entries = deviation * jax.random.normal(own_key, shape, jnp.float32)
    if shards:
        entries = entries * shard_levels(own_key, shape, shards, -0.22, 0.18)
    return jnp.clip(entries, -bound, bound).astype(kind)


def setup_inputs(seed: int = 0) -> dict:
    key_list = jax.random.split(jax.random.key(seed), 8)
    queries = draw_queries(jax.random.fold_in(key_list[7], 71), 0)
    keys = draw_keys(jax.random.fold_in(key_list[7], 71), 0)
    values = scatter_about(key_list[2], (NF, NR, COLS, D), 1.0, 6.0, ((0, 32), (1, 16)))
    grad_out = scatter_about(key_list[3], (NF, NR, COLS, D), 1.0, 6.0, ((0, 32), (1, 16)))
    window_radius = draw_window_radius(jax.random.fold_in(key_list[7], 71), 0)
    frames_valid = draw_frames_valid(jax.random.fold_in(key_list[7], 71), 0)
    rows_valid = draw_rows_valid(jax.random.fold_in(key_list[7], 71), 0)
    return {"queries": queries, "keys": keys, "values": values, "grad_out": grad_out, "window_radius": window_radius, "frames_valid": frames_valid, "rows_valid": rows_valid}


masked_score = -1.0e30


def tile_masks(radius, frame_counts, row_counts, frames, rows, columns):
    frame_pos = jnp.arange(3 * frames, dtype=jnp.int32)
    row_pos = jnp.arange(3 * rows, dtype=jnp.int32)
    frame_tile = frame_pos // frames
    row_tile = row_pos // rows
    tile_slots = jnp.arange(3, dtype=jnp.int32)
    pick_frame = (frame_tile[:, None] == tile_slots[None, :]).astype(jnp.int32)
    pick_row = (row_tile[:, None] == tile_slots[None, :]).astype(jnp.int32)
    frame_limit = jnp.dot(jnp.dot(pick_frame, frame_counts), pick_row.T)
    row_limit = jnp.dot(jnp.dot(pick_frame, row_counts), pick_row.T)
    inside = ((frame_pos % frames)[:, None] < frame_limit) & ((row_pos % rows)[None, :] < row_limit)
    within_reach = (jnp.abs(frame_tile - 1)[None, :, None] <= radius[:, 0][:, None, None]) & (
        jnp.abs(row_tile - 1)[None, None, :] <= radius[:, 1][:, None, None])
    flag_grid = within_reach & inside[None]
    return jnp.broadcast_to(flag_grid[..., None], flag_grid.shape + (columns,)).reshape(radius.shape[0], -1)


def both_counts(frame_line, row_line):
    frame_grid = frame_line[:, None] * (row_line[None, :] > 0).astype(jnp.int32)
    row_grid = row_line[None, :] * (frame_line[:, None] > 0).astype(jnp.int32)
    return frame_grid, row_grid


def clip_keep(tile_time, tile_row):
    offsets = jnp.arange(3, dtype=jnp.int32) - 1
    keep_time = ((tile_time + offsets) // CLIP_TT == tile_time // CLIP_TT).astype(jnp.int32)
    keep_row = ((tile_row + offsets) // CLIP_HT == tile_row // CLIP_HT).astype(jnp.int32)
    return keep_time, keep_row


def lowered(tensor):
    return lax.optimization_barrier(tensor.astype(jnp.bfloat16)).astype(jnp.float32)


def attend_tile(query, key_window, value_window, grad, key_allowed):
    query_count = query.shape[0]
    key_count = key_window.shape[0]
    width = query.shape[1]
    score_scale = HD ** -0.5
    query_heads = query.reshape(query_count, HEADS, HD).astype(jnp.float32)
    key_heads = key_window.reshape(key_count, HEADS, HD).astype(jnp.float32)
    value_heads = value_window.reshape(key_count, HEADS, HD).astype(jnp.float32)
    grad_heads = grad.reshape(query_count, HEADS, HD).astype(jnp.float32)
    allowed = key_allowed[:, None, :]
    scores = jnp.einsum("qhd,khd->hqk", query_heads, key_heads) * score_scale
    scores = jnp.where(allowed, scores, masked_score)
    row_max = jnp.max(scores, axis=2, keepdims=True)
    raised = jnp.exp(scores - row_max)
    totals = jnp.sum(raised, axis=2, keepdims=True)
    weights = raised / totals
    weights_low = lowered(weights)
    output = lowered(jnp.einsum("hqk,khd->qhd", weights_low, value_heads))
    row_delta = jnp.einsum("qhd,qhd->hq", grad_heads, output)
    grad_weights = jnp.einsum("qhd,khd->hqk", grad_heads, value_heads)
    grad_low = lowered(weights * (grad_weights - row_delta[:, :, None]))
    grad_query = jnp.einsum("hqk,khd->qhd", grad_low, key_heads) * score_scale
    grad_key = jnp.einsum("hqk,qhd->khd", grad_low, query_heads) * score_scale
    grad_value = jnp.einsum("hqk,qhd->khd", weights_low, grad_heads)

    def as_tiles(tensor):
        return tensor.reshape(3, TF, 3, TR, COLS, width).transpose(0, 2, 1, 3, 4, 5).reshape(
            3, 3, query_count, width).astype(jnp.bfloat16)

    return (grad_query.reshape(query_count, width).astype(jnp.bfloat16),
            as_tiles(grad_key), as_tiles(grad_value))


def reference(queries, keys, values, grad_out, window_radius, frames_valid, rows_valid):
    time_tiles = frames_valid.shape[0]
    row_tiles = rows_valid.shape[0]
    width = HEADS * HD
    query_count = TF * TR * COLS
    zero_index = jnp.int32(0)

    def padded(tensor):
        return jnp.pad(tensor, ((TF, TF), (TR, TR), (0, 0), (0, 0)))

    key_pad = padded(keys)
    value_pad = padded(values)
    frame_pad = jnp.pad(frames_valid, 1)
    row_pad = jnp.pad(rows_valid, 1)

    def window(tensor, tile_time, tile_row):
        start = (tile_time * TF, tile_row * TR, zero_index, zero_index)
        block = lax.dynamic_slice(tensor, start, (3 * TF, 3 * TR, COLS, tensor.shape[3]))
        return block.reshape(9 * query_count, tensor.shape[3])

    def own_block(tensor, tile_time, tile_row):
        start = (tile_time * TF, tile_row * TR, zero_index, zero_index)
        return lax.dynamic_slice(tensor, start, (TF, TR, COLS, width)).reshape(query_count, width)

    def one_tile(tile_time, tile_row):
        keep_time, keep_row = clip_keep(tile_time, tile_row)
        frame_line = lax.dynamic_slice(frame_pad, (tile_time,), (3,)) * keep_time
        row_line = lax.dynamic_slice(row_pad, (tile_row,), (3,)) * keep_row
        frame_grid, row_grid = both_counts(frame_line, row_line)
        key_allowed = tile_masks(window_radius, frame_grid, row_grid, TF, TR, COLS)
        return attend_tile(own_block(queries, tile_time, tile_row), window(key_pad, tile_time, tile_row),
                           window(value_pad, tile_time, tile_row), own_block(grad_out, tile_time, tile_row),
                           key_allowed)

    def gather_rows(part):
        part_pad = jnp.pad(part, ((1, 1), (0, 0), (0, 0), (0, 0), (0, 0)))
        total = (part_pad[2:, :, 0].astype(jnp.float32) + part_pad[1:-1, :, 1].astype(jnp.float32)
                 + part_pad[:-2, :, 2].astype(jnp.float32))
        return lowered(total).transpose(1, 0, 2, 3)

    def time_step(carry, tile_time):
        key_sum, value_sum = carry

        def row_task(tile_row):
            return one_tile(tile_time, tile_row)

        grad_query, key_part, value_part = lax.map(row_task, jnp.arange(row_tiles, dtype=jnp.int32))
        start = (tile_time, zero_index, zero_index, zero_index)
        extent = (3, row_tiles, query_count, width)
        key_sum = lax.dynamic_update_slice(key_sum, lax.dynamic_slice(key_sum, start, extent)
                                           + gather_rows(key_part), start)
        value_sum = lax.dynamic_update_slice(value_sum, lax.dynamic_slice(value_sum, start, extent)
                                             + gather_rows(value_part), start)
        return (key_sum, value_sum), grad_query

    empty = jnp.zeros((time_tiles + 2, row_tiles, query_count, width), jnp.float32)
    sums, grad_query = lax.scan(time_step, (empty, empty), jnp.arange(time_tiles, dtype=jnp.int32))

    def to_grid(tensor):
        return tensor.reshape(time_tiles, row_tiles, TF, TR, COLS, width).transpose(0, 2, 1, 3, 4, 5).reshape(
            NF, NR, COLS, width)

    return (to_grid(grad_query), to_grid(sums[0][1:-1].astype(jnp.bfloat16)),
            to_grid(sums[1][1:-1].astype(jnp.bfloat16)))
```

```python
import functools

import jax
import jax.numpy as jnp
from jax import lax
from jax.experimental import pallas as pl
from jax.experimental.pallas import tpu as pltpu
from jax.sharding import PartitionSpec as P

HEADS = 12
HD = 128
SLOTS = HEADS // 2
MESH = pl.DeviceIdType.MESH
F32 = jnp.float32
BF16 = jnp.bfloat16
LOG2E = 1.4426950408889634
MASKED = -1e30


def contract(lhs, rhs, lhs_dim, rhs_dim):
    return lax.dot_general(
        lhs, rhs, (((lhs_dim,), (rhs_dim,)), ((), ())), preferred_element_type=F32
    )


def key_bias(frame_counts, row_counts, time_reach, row_reach, n_time, n_row, frames, rows, tokens):
    count = n_time * n_row * tokens
    lane = lax.broadcasted_iota(jnp.int32, (1, count), 1)

    def steps(position, step, limit):
        total = jnp.zeros_like(position)
        for k in range(1, limit):
            total = total + jnp.where(position >= k * step, 1, 0)
        return total

    time_tile = steps(lane, n_row * tokens, n_time)
    in_time = lane - time_tile * (n_row * tokens)
    row_tile = steps(in_time, tokens, n_row)
    token = in_time - row_tile * tokens
    frame = steps(token, tokens // frames, frames)
    row = lane & (rows - 1)

    def picked(tile, counts, reach):
        if len(counts) == 1:
            return counts[0]
        outer = jnp.where(reach > 0, 1, 0)
        return jnp.where(
            tile == 1, counts[1], jnp.where(tile == 0, counts[0], counts[2]) * outer
        )

    inside = (frame < picked(time_tile, frame_counts, time_reach)) & (
        row < picked(row_tile, row_counts, row_reach)
    )
    return jnp.where(inside, 0.0, MASKED).astype(F32)


def attend(query, key, value, grad, bias):
    scale = HD**-0.5
    scores = contract(query, key, 1, 1) + bias
    row_max = jnp.max(scores, axis=1, keepdims=True)
    raised = jnp.exp2((scores - row_max) * (scale * LOG2E))
    weights = raised * (1.0 / jnp.sum(raised, axis=1, keepdims=True))
    weights_low = weights.astype(BF16)
    output = contract(weights_low, value, 1, 0).astype(BF16).astype(F32)
    row_delta = jnp.sum(output * grad.astype(F32), axis=1, keepdims=True)
    grad_weights = contract(grad, value, 1, 1)
    grad_low = (weights * (grad_weights - row_delta)).astype(BF16)
    grad_query = contract(grad_low, key, 1, 0) * scale
    grad_key = contract(grad_low, query, 0, 0) * scale
    grad_value = contract(weights_low, grad, 0, 0)
    return grad_query, grad_key, grad_value


def kernel(
    full, high, dims,
    perm, place, radius, fv, rv, q_in, k_in, v_in, g_in, dq_out, dk_out, dv_out,
    qg, kv, part, ret_y, ret_z, z_out, sums, result, stage, heads, frame_counts, row_counts,
    swap_s, swap_r, z_s, z_r, y_s, y_r, c_s, c_r, ry_s, ry_r, rz_s, rz_r, back_s, back_r,
    n_s, n_r,
):
    frames, rows, tokens, n_tm, n_height = dims
    tm = lax.axis_index("tm")
    height = lax.axis_index("height")
    chip = tm // 2
    core = tm % 2
    other = 1 - core
    sibling = (chip * 2 + other, height)
    z_next = ((tm + 2) % n_tm, height)
    z_prev = ((tm + n_tm - 2) % n_tm, height)
    y_next = (tm, (height + 1) % n_height)
    y_prev = (tm, (height + n_height - 1) % n_height)
    z_dev = (z_next, z_prev)
    y_dev = (y_next, y_prev)
    mid = pl.ds(tokens, tokens)

    def remote(src, dst, send, recv, device):
        return pltpu.make_async_remote_copy(
            src_ref=src, dst_ref=dst, send_sem=send, recv_sem=recv,
            device_id=device, device_id_type=MESH,
        )

    barrier = pltpu.get_barrier_semaphore()
    for device in (sibling, z_next, z_prev, y_next, y_prev):
        pl.semaphore_signal(barrier, inc=1, device_id=device, device_id_type=MESH)

    frame_counts[1 + core] = jnp.full((8, 128), fv[0], jnp.int32)
    row_counts[1] = jnp.full((8, 128), rv[0], jnp.int32)

    for head in range(HEADS):
        lanes = pl.ds(head * HD, HD)
        for index, source in enumerate((k_in, v_in, q_in, g_in)):
            heads[head, index] = source[:, lanes]

    def pack(slot, _):
        theirs = perm[2 * slot + other]
        mine = perm[2 * slot + core]
        stage[slot] = heads[theirs]
        block = heads[mine]
        kv[slot, 0, 1 + core, mid] = block[0]
        kv[slot, 1, 1 + core, mid] = block[1]
        qg[slot, 0, core] = block[2]
        qg[slot, 1, core] = block[3]
        return 0

    lax.fori_loop(0, SLOTS, pack, 0)
    pl.semaphore_wait(barrier, 5)

    def counts_swap():
        return remote(
            frame_counts.at[1 + core], frame_counts.at[1 + core], n_s.at[0], n_r.at[0], sibling
        )

    def counts_z(way):
        return remote(
            frame_counts.at[2 - way], frame_counts.at[3 * way], n_s.at[1 + way], n_r.at[1 + way],
            z_dev[way],
        )

    def counts_y(way):
        return remote(
            row_counts.at[1], row_counts.at[2 * way], n_s.at[3 + way], n_r.at[3 + way], y_dev[way]
        )

    def swap_kv(slot):
        return remote(
            stage.at[slot, pl.ds(0, 2)], kv.at[slot, :, 1 + core, mid], swap_s.at[0, slot],
            swap_r.at[0, slot], sibling,
        )

    def swap_qg(slot):
        return remote(
            stage.at[slot, pl.ds(2, 2)], qg.at[slot, :, core], swap_s.at[1, slot],
            swap_r.at[1, slot], sibling,
        )

    def send_z(slot, way):
        return remote(
            kv.at[slot, :, 2 - way, mid], kv.at[slot, :, 3 * way, mid], z_s.at[way, slot],
            z_r.at[way, slot], z_dev[way],
        )

    def send_y(slot, way):
        return remote(
            kv.at[slot, :, pl.ds(1, 2), mid],
            kv.at[slot, :, pl.ds(1, 2), pl.ds(2 * way * tokens, tokens)],
            y_s.at[way, slot], y_r.at[way, slot], y_dev[way],
        )

    def send_corner(slot, way, side):
        return remote(
            kv.at[slot, :, 3 * side, mid],
            kv.at[slot, :, 3 * side, pl.ds(2 * way * tokens, tokens)],
            c_s.at[way, side, slot], c_r.at[way, side, slot], y_dev[way],
        )

    def return_y(slot, way, time):
        return remote(
            part.at[slot, :, time, pl.ds(2 * (1 - way) * tokens, tokens)],
            ret_y.at[way, slot, :, time],
            ry_s.at[way, slot], ry_r.at[way, slot], y_dev[way],
        )

    def return_z(slot, way):
        return remote(
            z_out.at[way, slot], ret_z.at[way, slot], rz_s.at[way, slot], rz_r.at[way, slot],
            z_dev[way],
        )

    def send_back(slot):
        return remote(
            result.at[2 * SLOTS + slot], result.at[core * SLOTS + slot], back_s.at[slot], back_r.at[slot], sibling
        )

    counts_swap().start()
    for way in range(2):
        counts_y(way).start()

    def loop(start, stop, body):
        if stop > start:
            def step(slot, _):
                body(slot)
                return 0
            lax.fori_loop(start, stop, step, 0)

    loop(0, SLOTS, lambda slot: swap_kv(slot).start())
    loop(0, SLOTS, lambda slot: swap_qg(slot).start())
    counts_swap().wait_recv()
    for way in range(2):
        counts_z(way).start()

    def first_full(slot):
        swap_kv(slot).wait_recv()
        for way in range(2):
            send_z(slot, way).start()
        for way in range(2):
            send_y(slot, way).start()

    def first_high(slot):
        swap_kv(slot).wait_recv()
        for way in range(2):
            send_y(slot, way).start()

    def first_wide(slot):
        swap_kv(slot).wait_recv()
        for way in range(2):
            send_z(slot, way).start()

    loop(0, full, first_full)
    loop(high, SLOTS, first_wide)
    loop(full, high, first_high)

    def corners(slot):
        for side in range(2):
            send_z(slot, side).wait_recv()
            for way in range(2):
                send_corner(slot, way, side).start()

    loop(0, full, corners)

    for way in range(2):
        counts_z(way).wait_recv()
        counts_y(way).wait_recv()

    edges_time = (
        jnp.where(chip > 0, 1, 0), 1, 1, jnp.where(chip < n_tm // 2 - 1, 1, 0)
    )
    edges_row = (
        jnp.where(height > 0, 1, 0), 1, jnp.where(height < n_height - 1, 1, 0)
    )

    def frame_count(time):
        return frame_counts[time, 0:1, 0:1] * edges_time[time]

    def row_count(row):
        return row_counts[row, 0:1, 0:1] * edges_row[row]

    def compute(slot, n_time, n_row):
        time_reach, row_reach = radius[0, 2 * slot + core], radius[1, 2 * slot + core]
        swap_qg(slot).wait_recv()
        first_row = 0 if n_row == 3 else 1
        key_parts = []
        value_parts = []
        for tile in range(2):
            first_time = tile if n_time == 3 else tile + 1
            bias = key_bias(
                [frame_count(first_time + k) for k in range(n_time)],
                [row_count(first_row + k) for k in range(n_row)],
                time_reach, row_reach, n_time, n_row, frames, rows, tokens,
            )
            span = (pl.ds(first_time, n_time), pl.ds(first_row * tokens, n_row * tokens))
            count = n_time * n_row * tokens
            key = kv[slot, 0, span[0], span[1]].reshape(count, HD)
            value = kv[slot, 1, span[0], span[1]].reshape(count, HD)
            grad_query, grad_key, grad_value = attend(
                qg[slot, 0, tile], key, value, qg[slot, 1, tile], bias
            )
            low = grad_query.astype(BF16)

            @pl.when(core == tile)
            def _(low=low):
                result[core * SLOTS + slot, 0] = low

            @pl.when(core != tile)
            def _(low=low):
                result[2 * SLOTS + slot, 0] = low

            key_parts.append(grad_key)
            value_parts.append(grad_value)
        where = pl.ds(first_row * tokens, n_row * tokens)
        width = n_row * tokens
        for kind, parts in ((0, key_parts), (1, value_parts)):
            if n_time == 3:
                part[slot, kind, 0, where] = parts[0][:width].astype(BF16)
                for time in (1, 2):
                    part[slot, kind, time, where] = (
                        parts[0][time * width : (time + 1) * width]
                        + parts[1][(time - 1) * width : time * width]
                    ).astype(BF16)
                part[slot, kind, 3, where] = parts[1][2 * width :].astype(BF16)
            else:
                part[slot, kind, 1, where] = parts[0].astype(BF16)
                part[slot, kind, 2, where] = parts[1].astype(BF16)

    every = pl.ds(0, 4)
    own = pl.ds(1, 2)

    def compute_full(slot):
        for way in range(2):
            send_y(slot, way).wait_recv()
            for side in range(2):
                send_corner(slot, way, side).wait_recv()
        compute(slot, 3, 3)
        for way in range(2):
            return_y(slot, way, every).start()

    def compute_high(slot):
        for way in range(2):
            send_y(slot, way).wait_recv()
        compute(slot, 1, 3)
        for way in range(2):
            return_y(slot, way, own).start()

    def compute_wide(slot):
        for way in range(2):
            send_z(slot, way).wait_recv()
        compute(slot, 3, 1)
        for kind in range(2):
            for time in (1, 2):
                sums[slot, kind, time - 1] = part[slot, kind, time, mid].astype(F32)
            z_out[0, slot, kind] = part[slot, kind, 3, mid]
            z_out[1, slot, kind] = part[slot, kind, 0, mid]
        for way in range(2):
            return_z(slot, way).start()

    loop(high, SLOTS, compute_wide)
    loop(0, full, compute_full)
    loop(full, high, compute_high)

    def reduced(slot, kind, time):
        return (
            part[slot, kind, time, mid].astype(F32)
            + ret_y[0, slot, kind, time].astype(F32)
            + ret_y[1, slot, kind, time].astype(F32)
        )

    def reduce_full(slot):
        for way in range(2):
            return_y(slot, way, every).wait_recv()
        for kind in range(2):
            for time in (1, 2):
                sums[slot, kind, time - 1] = reduced(slot, kind, time)
            z_out[0, slot, kind] = reduced(slot, kind, 3).astype(BF16)
            z_out[1, slot, kind] = reduced(slot, kind, 0).astype(BF16)
        for way in range(2):
            return_z(slot, way).start()

    def reduce_high(slot):
        for way in range(2):
            return_y(slot, way, own).wait_recv()
        for kind in range(2):
            for time in (1, 2):
                sums[slot, kind, time - 1] = reduced(slot, kind, time)

    loop(0, full, reduce_full)
    loop(full, high, reduce_high)

    def finish(slot, with_z):
        if with_z:
            for way in range(2):
                return_z(slot, way).wait_recv()
        for kind in range(2):
            for tile in range(2):
                total = sums[slot, kind, tile]
                if with_z:
                    total = total + ret_z[tile, slot, kind].astype(F32)
                low = total.astype(BF16)

                @pl.when(core == tile)
                def _(low=low, kind=kind):
                    result[core * SLOTS + slot, 1 + kind] = low

                @pl.when(core != tile)
                def _(low=low, kind=kind):
                    result[2 * SLOTS + slot, 1 + kind] = low

        send_back(slot).start()

    loop(full, high, lambda slot: finish(slot, False))
    loop(high, SLOTS, lambda slot: finish(slot, True))
    loop(0, full, lambda slot: finish(slot, True))

    def drain(slot):
        swap_kv(slot).wait_send()
        swap_qg(slot).wait_send()
        send_back(slot).wait_send()

    def drain_z(slot):
        for way in range(2):
            send_z(slot, way).wait_send()
            return_z(slot, way).wait_send()

    def drain_y(slot, time):
        for way in range(2):
            send_y(slot, way).wait_send()
            return_y(slot, way, time).wait_send()

    def drain_corner(slot):
        for way in range(2):
            for side in range(2):
                send_corner(slot, way, side).wait_send()

    loop(0, SLOTS, drain)
    loop(0, full, drain_z)
    loop(high, SLOTS, drain_z)
    loop(0, full, lambda slot: drain_y(slot, every))
    loop(full, high, lambda slot: drain_y(slot, own))
    loop(0, full, drain_corner)
    counts_swap().wait_send()
    for way in range(2):
        counts_z(way).wait_send()
        counts_y(way).wait_send()

    loop(0, SLOTS, lambda slot: send_back(slot).wait_recv())

    for head in range(HEADS):
        lanes = pl.ds(head * HD, HD)
        where = place[head]
        block = result[where]
        dq_out[:, lanes] = block[0]
        dk_out[:, lanes] = block[1]
        dv_out[:, lanes] = block[2]


def tile_call(full, high, dims, collective_id, operands):
    frames, rows, tokens, n_tm, n_height = dims
    width = HEADS * HD
    smem = pl.BlockSpec(memory_space=pltpu.SMEM)
    vmem = pl.BlockSpec(memory_space=pltpu.VMEM)
    dma = pltpu.SemaphoreType.DMA
    tile = (tokens, HD)
    out = jax.ShapeDtypeStruct((tokens, width), BF16)
    return pl.pallas_call(
        functools.partial(kernel, full, high, dims),
        out_shape=(out, out, out),
        in_specs=[smem] * 5 + [vmem] * 4,
        out_specs=(vmem, vmem, vmem),
        scratch_shapes=[
            pltpu.VMEM((SLOTS, 2, 2) + tile, BF16),
            pltpu.VMEM((SLOTS, 2, 4, 3 * tokens, HD), BF16),
            pltpu.VMEM((SLOTS, 2, 4, 3 * tokens, HD), BF16),
            pltpu.VMEM((2, SLOTS, 2, 4) + tile, BF16),
            pltpu.VMEM((2, SLOTS, 2) + tile, BF16),
            pltpu.VMEM((2, SLOTS, 2) + tile, BF16),
            pltpu.VMEM((SLOTS, 2, 2) + tile, F32),
            pltpu.VMEM((3 * SLOTS, 3) + tile, BF16),
            pltpu.VMEM((SLOTS, 4) + tile, BF16),
            pltpu.VMEM((HEADS, 4) + tile, BF16),
            pltpu.VMEM((4, 8, 128), jnp.int32),
            pltpu.VMEM((3, 8, 128), jnp.int32),
            dma((2, SLOTS)), dma((2, SLOTS)),
            dma((2, SLOTS)), dma((2, SLOTS)),
            dma((2, SLOTS)), dma((2, SLOTS)),
            dma((2, 2, SLOTS)), dma((2, 2, SLOTS)),
            dma((2, SLOTS)), dma((2, SLOTS)),
            dma((2, SLOTS)), dma((2, SLOTS)),
            dma((SLOTS,)), dma((SLOTS,)),
            dma((5,)), dma((5,)),
        ],
        compiler_params=pltpu.CompilerParams(
            collective_id=collective_id, has_side_effects=True, vmem_limit_bytes=56 << 20
        ),
        cost_estimate=pl.CostEstimate(
            flops=2 * 6 * tokens * 9 * tokens * width, bytes_accessed=7 * 2 * tokens * width,
            transcendentals=9 * tokens * tokens * HEADS,
        ),
    )(*operands)


def on_device(queries, keys, values, grad_out, window_radius, frames_valid, rows_valid):
    frames, rows, columns, width = queries.shape
    tokens = frames * rows * columns

    def flat(block):
        return block.transpose(0, 2, 1, 3).reshape(tokens, width)

    def unflat(block):
        return block.reshape(frames, columns, rows, width).transpose(0, 2, 1, 3)

    dims = (frames, rows, tokens, lax.axis_size("tm"), lax.axis_size("height"))
    time_reach, row_reach = window_radius[:, 0], window_radius[:, 1]
    kind = jnp.where(row_reach > 0, 1 - time_reach, 2 + time_reach)
    heads = jnp.arange(HEADS, dtype=jnp.int32)
    order = kind * HEADS + heads
    rank = jnp.sum((order[None, :] < order[:, None]).astype(jnp.int32), axis=1)
    perm = jnp.sum(jnp.where(rank[None, :] == heads[:, None], heads[None, :], 0), axis=1)
    reach = jnp.sum(
        jnp.where(rank[None, None, :] == heads[None, :, None], window_radius.T[:, None, :], 0), axis=2
    )
    place = (rank % 2) * SLOTS + rank // 2
    operands = (
        perm, place, reach, frames_valid, rows_valid,
        flat(queries), flat(keys), flat(values), flat(grad_out),
    )
    outs = tile_call(SLOTS, SLOTS, dims, 0, operands)
    return tuple(unflat(out) for out in outs)


def solution(mesh):
    placed = P("tm", "height", None, None)
    return jax.shard_map(
        on_device,
        mesh=mesh,
        in_specs=(placed, placed, placed, placed, P(), P("tm"), P("height")),
        out_specs=(placed, placed, placed),
        check_vma=False,
    )
```

```python
import functools

import jax
import jax.numpy as jnp
from jax import lax
from jax.experimental import pallas as pl
from jax.experimental.pallas import tpu as pltpu
from jax.sharding import PartitionSpec as P

HEADS = 12
HD = 128
SLOTS = HEADS // 2
PLANS = ((2, 4), (3, 5), (SLOTS, SLOTS))
MESH = pl.DeviceIdType.MESH
F32 = jnp.float32
BF16 = jnp.bfloat16
LOG2E = 1.4426950408889634
MASKED = -1e30


def contract(lhs, rhs, lhs_dim, rhs_dim):
    return lax.dot_general(
        lhs, rhs, (((lhs_dim,), (rhs_dim,)), ((), ())), preferred_element_type=F32
    )


def key_bias(frame_counts, row_counts, time_reach, row_reach, n_time, n_row, frames, rows, tokens):
    count = n_time * n_row * tokens
    lane = lax.broadcasted_iota(jnp.int32, (1, count), 1)

    def steps(position, step, limit):
        total = jnp.zeros_like(position)
        for k in range(1, limit):
            total = total + jnp.where(position >= k * step, 1, 0)
        return total

    time_tile = steps(lane, n_row * tokens, n_time)
    in_time = lane - time_tile * (n_row * tokens)
    row_tile = steps(in_time, tokens, n_row)
    token = in_time - row_tile * tokens
    frame = steps(token, tokens // frames, frames)
    row = lane & (rows - 1)

    def picked(tile, counts, reach):
        if len(counts) == 1:
            return counts[0]
        outer = jnp.where(reach > 0, 1, 0)
        return jnp.where(
            tile == 1, counts[1], jnp.where(tile == 0, counts[0], counts[2]) * outer
        )

    inside = (frame < picked(time_tile, frame_counts, time_reach)) & (
        row < picked(row_tile, row_counts, row_reach)
    )
    return jnp.where(inside, 0.0, MASKED).astype(F32)


def attend(query, key, value, grad, bias):
    scale = HD**-0.5
    scores = contract(query, key, 1, 1) + bias
    row_max = jnp.max(scores, axis=1, keepdims=True)
    raised = jnp.exp2((scores - row_max) * (scale * LOG2E))
    weights = raised * (1.0 / jnp.sum(raised, axis=1, keepdims=True))
    weights_low = weights.astype(BF16)
    output = contract(weights_low, value, 1, 0).astype(BF16).astype(F32)
    row_delta = jnp.sum(output * grad.astype(F32), axis=1, keepdims=True)
    grad_weights = contract(grad, value, 1, 1)
    grad_low = (weights * (grad_weights - row_delta)).astype(BF16)
    grad_query = contract(grad_low, key, 1, 0) * scale
    grad_key = contract(grad_low, query, 0, 0) * scale
    grad_value = contract(weights_low, grad, 0, 0)
    return grad_query, grad_key, grad_value


def kernel(
    full, high, dims,
    perm, place, radius, fv, rv, q_in, k_in, v_in, g_in, dq_out, dk_out, dv_out,
    qg, kv, part, ret_y, ret_z, z_out, sums, result, stage, heads, frame_counts, row_counts,
    swap_s, swap_r, z_s, z_r, y_s, y_r, ry_s, ry_r, rz_s, rz_r, back_s, back_r,
    n_s, n_r,
):
    frames, rows, tokens, n_tm, n_height = dims
    tm = lax.axis_index("tm")
    height = lax.axis_index("height")
    chip = tm // 2
    core = tm % 2
    other = 1 - core
    sibling = (chip * 2 + other, height)
    z_next = ((tm + 2) % n_tm, height)
    z_prev = ((tm + n_tm - 2) % n_tm, height)
    y_next = (tm, (height + 1) % n_height)
    y_prev = (tm, (height + n_height - 1) % n_height)
    z_dev = (z_next, z_prev)
    y_dev = (y_next, y_prev)
    half = n_height // 2
    relay = (height == n_height - 1, height == 0)
    entry = (height == half - 1, height == half)
    far = (
        (tm, jnp.where(entry[0], n_height - 1, jnp.where(relay[0], half, height + 1))),
        (tm, jnp.where(entry[1], 0, jnp.where(relay[1], half - 1, height - 1))),
    )
    land = (jnp.where(entry[0], 1, 0), jnp.where(entry[1], 0, 1))
    origin = (jnp.where(relay[0], 2, 1), jnp.where(relay[1], 0, 1))
    special = relay[0] | relay[1] | entry[0] | entry[1]
    upper = height >= half
    at_end = relay[0] | relay[1]
    greet_first = jnp.where(at_end, jnp.where(upper, half - 1, half), jnp.where(upper, 0, n_height - 1))
    greet_second = jnp.where(at_end, jnp.where(upper, half, half - 1), jnp.where(upper, n_height - 1, 0))

    def remote(src, dst, send, recv, device):
        return pltpu.make_async_remote_copy(
            src_ref=src, dst_ref=dst, send_sem=send, recv_sem=recv,
            device_id=device, device_id_type=MESH,
        )

    barrier = pltpu.get_barrier_semaphore()
    for device in (sibling, z_next, z_prev, y_next, y_prev):
        pl.semaphore_signal(barrier, inc=1, device_id=device, device_id_type=MESH)

    @pl.when(special)
    def _():
        for device in ((tm, greet_first), (tm, greet_second)):
            pl.semaphore_signal(barrier, inc=1, device_id=device, device_id_type=MESH)

    frame_counts[1 + core] = jnp.full((8, 128), fv[0], jnp.int32)
    row_counts[1] = jnp.full((8, 128), rv[0], jnp.int32)

    for head in range(HEADS):
        lanes = pl.ds(head * HD, HD)
        for index, source in enumerate((k_in, v_in, q_in, g_in)):
            heads[head, index] = source[:, lanes]

    def pack(slot, _):
        theirs = perm[2 * slot + other]
        mine = perm[2 * slot + core]
        stage[slot] = heads[theirs]
        block = heads[mine]
        kv[slot, 0, 1 + core, 1] = block[0]
        kv[slot, 1, 1 + core, 1] = block[1]
        qg[slot, 0, core] = block[2]
        qg[slot, 1, core] = block[3]
        return 0

    lax.fori_loop(0, SLOTS, pack, 0)

    for way in range(2):
        @pl.when(relay[way])
        def _(way=way):
            def clear(slot, _):
                kv[slot, 0, :, 2 * (1 - way)] = jnp.zeros((4, tokens, HD), BF16)
                return 0

            lax.fori_loop(0, SLOTS, clear, 0)

    @pl.when(special)
    def _():
        pl.semaphore_wait(barrier, 7)

    @pl.when(jnp.logical_not(special))
    def _():
        pl.semaphore_wait(barrier, 5)

    def counts_swap():
        return remote(
            frame_counts.at[1 + core], frame_counts.at[1 + core], n_s.at[0], n_r.at[0], sibling
        )

    def counts_z(way):
        return remote(
            frame_counts.at[2 - way], frame_counts.at[3 * way], n_s.at[1 + way], n_r.at[1 + way],
            z_dev[way],
        )

    def counts_y(way):
        return remote(
            row_counts.at[1], row_counts.at[2 * way], n_s.at[3 + way], n_r.at[3 + way], y_dev[way]
        )

    def swap_kv(slot):
        return remote(
            stage.at[slot, pl.ds(0, 2)], kv.at[slot, :, 1 + core, 1], swap_s.at[0, slot],
            swap_r.at[0, slot], sibling,
        )

    def swap_qg(slot):
        return remote(
            stage.at[slot, pl.ds(2, 2)], qg.at[slot, :, core], swap_s.at[1, slot],
            swap_r.at[1, slot], sibling,
        )

    def send_z(slot, way):
        return remote(
            kv.at[slot, :, 2 - way, 1], kv.at[slot, :, 3 * way, 1], z_s.at[way, slot],
            z_r.at[way, slot], z_dev[way],
        )

    times = (pl.ds(1, 2), pl.ds(0, 1), pl.ds(3, 1))

    def send_y(slot, way, kind, group):
        time = times[group]
        start, stop, device = (1, way, y_dev[way]) if kind == 0 else (origin[way], land[way], far[way])
        return remote(
            kv.at[slot, kind, time, start], kv.at[slot, kind, time, 2 * stop],
            y_s.at[group, kind, way, slot], y_r.at[group, kind, stop, slot], device,
        )

    def arrive_y(slot, way, kind, group):
        time = times[group]
        return remote(
            kv.at[slot, kind, time, 1], kv.at[slot, kind, time, 2 * way],
            y_s.at[group, kind, way, slot], y_r.at[group, kind, way, slot], y_dev[way],
        )

    def start_y(slot, group):
        for way in range(2):
            @pl.when(jnp.logical_not(relay[way]))
            def _(way=way):
                send_y(slot, way, 0, group).start()
                send_y(slot, way, 1, group).start()

        for way in range(2):
            @pl.when(relay[way])
            def _(way=way):
                arrive_y(slot, 1 - way, 1, group).wait_recv()
                send_y(slot, way, 1, group).start()

    def wait_y(slot, groups):
        for way in range(2):
            @pl.when(jnp.logical_not(relay[1 - way]))
            def _(way=way):
                for group in groups:
                    for kind in range(2):
                        arrive_y(slot, way, kind, group).wait_recv()

    def return_y(slot, way, kind, time):
        stop, device = (way, y_dev[way]) if kind == 0 else (land[way], far[way])
        return remote(
            part.at[slot, kind, time, 2 * (1 - way)], ret_y.at[stop, slot, kind, time],
            ry_s.at[kind, way, slot], ry_r.at[kind, stop, slot], device,
        )

    def returned_y(slot, way, kind, time):
        return remote(
            part.at[slot, kind, time, 2 * (1 - way)], ret_y.at[way, slot, kind, time],
            ry_s.at[kind, way, slot], ry_r.at[kind, way, slot], y_dev[way],
        )

    def relay_y(slot, way, time):
        return remote(
            ret_y.at[1 - way, slot, 1, time], ret_y.at[way, slot, 1, time],
            ry_s.at[1, way, slot], ry_r.at[1, way, slot], far[way],
        )

    def start_return(slot, time):
        for way in range(2):
            @pl.when(jnp.logical_not(relay[way]))
            def _(way=way):
                for kind in range(2):
                    return_y(slot, way, kind, time).start()

    def pass_return(slot, time):
        for way in range(2):
            @pl.when(relay[way])
            def _(way=way):
                returned_y(slot, 1 - way, 1, time).wait_recv()
                relay_y(slot, way, time).start()

    def wait_return(slot, time):
        for way in range(2):
            @pl.when(jnp.logical_not(relay[1 - way]))
            def _(way=way):
                for kind in range(2):
                    returned_y(slot, way, kind, time).wait_recv()

    def return_z(slot, way):
        return remote(
            z_out.at[way, slot], ret_z.at[way, slot], rz_s.at[way, slot], rz_r.at[way, slot],
            z_dev[way],
        )

    def send_back(slot):
        return remote(
            result.at[2 * SLOTS + slot], result.at[core * SLOTS + slot], back_s.at[slot],
            back_r.at[slot], sibling,
        )

    counts_swap().start()
    for way in range(2):
        counts_y(way).start()

    def loop(start, stop, body):
        if stop > start:
            def step(slot, _):
                body(slot)
                return 0
            lax.fori_loop(start, stop, step, 0)

    loop(0, SLOTS, lambda slot: swap_kv(slot).start())
    loop(0, SLOTS, lambda slot: swap_qg(slot).start())
    counts_swap().wait_recv()
    for way in range(2):
        counts_z(way).start()

    def first_z(slot):
        swap_kv(slot).wait_recv()
        for way in range(2):
            send_z(slot, way).start()

    loop(0, full, first_z)
    loop(full, high, lambda slot: swap_kv(slot).wait_recv())
    loop(high, SLOTS, first_z)
    if full:
        start_y(0, 0)

    def corners(slot):
        @pl.when(slot + 1 < full)
        def _():
            start_y(slot + 1, 0)

        for side in range(2):
            send_z(slot, side).wait_recv()
            start_y(slot, 1 + side)

    loop(0, full, corners)
    loop(full, high, lambda slot: start_y(slot, 0))

    for way in range(2):
        counts_z(way).wait_recv()
        counts_y(way).wait_recv()

    edges_time = (
        jnp.where(chip > 0, 1, 0), 1, 1, jnp.where(chip < n_tm // 2 - 1, 1, 0)
    )
    edges_row = (
        jnp.where(height > 0, 1, 0), 1, jnp.where(height < n_height - 1, 1, 0)
    )

    def frame_count(time):
        return frame_counts[time, 0:1, 0:1] * edges_time[time]

    def row_count(row):
        return row_counts[row, 0:1, 0:1] * edges_row[row]

    def compute(slot, n_time, n_row):
        time_reach, row_reach = radius[0, 2 * slot + core], radius[1, 2 * slot + core]
        swap_qg(slot).wait_recv()
        first_row = 0 if n_row == 3 else 1
        key_parts = []
        value_parts = []
        for tile in range(2):
            first_time = tile if n_time == 3 else tile + 1
            bias = key_bias(
                [frame_count(first_time + k) for k in range(n_time)],
                [row_count(first_row + k) for k in range(n_row)],
                time_reach, row_reach, n_time, n_row, frames, rows, tokens,
            )
            span = (pl.ds(first_time, n_time), pl.ds(first_row, n_row))
            count = n_time * n_row * tokens
            key = kv[slot, 0, span[0], span[1]].reshape(count, HD)
            value = kv[slot, 1, span[0], span[1]].reshape(count, HD)
            grad_query, grad_key, grad_value = attend(
                qg[slot, 0, tile], key, value, qg[slot, 1, tile], bias
            )
            low = grad_query.astype(BF16)

            @pl.when(core == tile)
            def _(low=low):
                result[core * SLOTS + slot, 0] = low

            @pl.when(core != tile)
            def _(low=low):
                result[2 * SLOTS + slot, 0] = low

            key_parts.append(grad_key)
            value_parts.append(grad_value)
        where = pl.ds(first_row, n_row)
        width = n_row * tokens

        def put(kind, time, total):
            part[slot, kind, time, where] = total.astype(BF16).reshape(n_row, tokens, HD)

        for kind, parts in ((0, key_parts), (1, value_parts)):
            if n_time == 3:
                put(kind, 0, parts[0][:width])
                for time in (1, 2):
                    put(
                        kind, time,
                        parts[0][time * width : (time + 1) * width]
                        + parts[1][(time - 1) * width : time * width],
                    )
                put(kind, 3, parts[1][2 * width :])
            else:
                put(kind, 1, parts[0])
                put(kind, 2, parts[1])

    every = pl.ds(0, 4)
    own = pl.ds(1, 2)

    def compute_full(slot):
        wait_y(slot, (0, 1, 2))
        compute(slot, 3, 3)
        start_return(slot, every)

        @pl.when(slot > 0)
        def _():
            pass_return(slot - 1, every)

    def compute_high(slot):
        wait_y(slot, (0,))
        compute(slot, 1, 3)
        start_return(slot, own)

        @pl.when(slot > full)
        def _():
            pass_return(slot - 1, own)

    def compute_wide(slot):
        for way in range(2):
            send_z(slot, way).wait_recv()
        compute(slot, 3, 1)
        for kind in range(2):
            for time in (1, 2):
                sums[slot, kind, time - 1] = part[slot, kind, time, 1].astype(F32)
            z_out[0, slot, kind] = part[slot, kind, 3, 1]
            z_out[1, slot, kind] = part[slot, kind, 0, 1]
        for way in range(2):
            return_z(slot, way).start()

    loop(high, SLOTS, compute_wide)
    loop(0, full, compute_full)
    if full:
        pass_return(full - 1, every)
    loop(full, high, compute_high)
    if high > full:
        pass_return(high - 1, own)

    def reduced(slot, kind, time):
        total = part[slot, kind, time, 1].astype(F32)
        for way in range(2):
            block = ret_y[way, slot, kind, time].astype(F32)
            total = total + jnp.where(relay[1 - way], 0.0, block)
        return total

    def reduce_full(slot):
        wait_return(slot, every)
        for kind in range(2):
            for time in (1, 2):
                sums[slot, kind, time - 1] = reduced(slot, kind, time)
            z_out[0, slot, kind] = reduced(slot, kind, 3).astype(BF16)
            z_out[1, slot, kind] = reduced(slot, kind, 0).astype(BF16)
        for way in range(2):
            return_z(slot, way).start()

    def reduce_high(slot):
        wait_return(slot, own)
        for kind in range(2):
            for time in (1, 2):
                sums[slot, kind, time - 1] = reduced(slot, kind, time)

    loop(0, full, reduce_full)
    loop(full, high, reduce_high)

    def finish(slot, with_z):
        if with_z:
            for way in range(2):
                return_z(slot, way).wait_recv()
        for kind in range(2):
            for tile in range(2):
                total = sums[slot, kind, tile]
                if with_z:
                    total = total + ret_z[tile, slot, kind].astype(F32)
                low = total.astype(BF16)

                @pl.when(core == tile)
                def _(low=low, kind=kind):
                    result[core * SLOTS + slot, 1 + kind] = low

                @pl.when(core != tile)
                def _(low=low, kind=kind):
                    result[2 * SLOTS + slot, 1 + kind] = low

        send_back(slot).start()

    loop(full, high, lambda slot: finish(slot, False))
    loop(high, SLOTS, lambda slot: finish(slot, True))
    loop(0, full, lambda slot: finish(slot, True))

    def drain(slot):
        swap_kv(slot).wait_send()
        swap_qg(slot).wait_send()
        send_back(slot).wait_send()

    def drain_z(slot):
        for way in range(2):
            send_z(slot, way).wait_send()
            return_z(slot, way).wait_send()

    def drain_y(slot, groups, time):
        for way in range(2):
            @pl.when(jnp.logical_not(relay[way]))
            def _(way=way):
                for group in groups:
                    send_y(slot, way, 0, group).wait_send()
                return_y(slot, way, 0, time).wait_send()

            for group in groups:
                send_y(slot, way, 1, group).wait_send()
            return_y(slot, way, 1, time).wait_send()

    loop(0, SLOTS, drain)
    loop(0, full, drain_z)
    loop(high, SLOTS, drain_z)
    loop(0, full, lambda slot: drain_y(slot, (0, 1, 2), every))
    loop(full, high, lambda slot: drain_y(slot, (0,), own))
    counts_swap().wait_send()
    for way in range(2):
        counts_z(way).wait_send()
        counts_y(way).wait_send()

    loop(0, SLOTS, lambda slot: send_back(slot).wait_recv())

    for head in range(HEADS):
        lanes = pl.ds(head * HD, HD)
        where = place[head]
        block = result[where]
        dq_out[:, lanes] = block[0]
        dk_out[:, lanes] = block[1]
        dv_out[:, lanes] = block[2]


def tile_call(full, high, dims, collective_id, operands):
    frames, rows, tokens, n_tm, n_height = dims
    width = HEADS * HD
    smem = pl.BlockSpec(memory_space=pltpu.SMEM)
    vmem = pl.BlockSpec(memory_space=pltpu.VMEM)
    dma = pltpu.SemaphoreType.DMA
    tile = (tokens, HD)
    out = jax.ShapeDtypeStruct((tokens, width), BF16)
    return pl.pallas_call(
        functools.partial(kernel, full, high, dims),
        out_shape=(out, out, out),
        in_specs=[smem] * 5 + [vmem] * 4,
        out_specs=(vmem, vmem, vmem),
        scratch_shapes=[
            pltpu.VMEM((SLOTS, 2, 2) + tile, BF16),
            pltpu.VMEM((SLOTS, 2, 4, 3) + tile, BF16),
            pltpu.VMEM((SLOTS, 2, 4, 3) + tile, BF16),
            pltpu.VMEM((2, SLOTS, 2, 4) + tile, BF16),
            pltpu.VMEM((2, SLOTS, 2) + tile, BF16),
            pltpu.VMEM((2, SLOTS, 2) + tile, BF16),
            pltpu.VMEM((SLOTS, 2, 2) + tile, F32),
            pltpu.VMEM((3 * SLOTS, 3) + tile, BF16),
            pltpu.VMEM((SLOTS, 4) + tile, BF16),
            pltpu.VMEM((HEADS, 4) + tile, BF16),
            pltpu.VMEM((4, 8, 128), jnp.int32),
            pltpu.VMEM((3, 8, 128), jnp.int32),
            dma((2, SLOTS)), dma((2, SLOTS)),
            dma((2, SLOTS)), dma((2, SLOTS)),
            dma((3, 2, 2, SLOTS)), dma((3, 2, 2, SLOTS)),
            dma((2, 2, SLOTS)), dma((2, 2, SLOTS)),
            dma((2, SLOTS)), dma((2, SLOTS)),
            dma((SLOTS,)), dma((SLOTS,)),
            dma((5,)), dma((5,)),
        ],
        compiler_params=pltpu.CompilerParams(
            collective_id=collective_id, has_side_effects=True, vmem_limit_bytes=56 << 20
        ),
        cost_estimate=pl.CostEstimate(
            flops=2 * 6 * tokens * 9 * tokens * width, bytes_accessed=7 * 2 * tokens * width,
            transcendentals=9 * tokens * tokens * HEADS,
        ),
    )(*operands)


def on_device(queries, keys, values, grad_out, window_radius, frames_valid, rows_valid):
    frames, rows, columns, width = queries.shape
    tokens = frames * rows * columns

    def flat(block):
        return block.transpose(0, 2, 1, 3).reshape(tokens, width)

    def unflat(block):
        return block.reshape(frames, columns, rows, width).transpose(0, 2, 1, 3)

    dims = (frames, rows, tokens, lax.axis_size("tm"), lax.axis_size("height"))
    time_reach, row_reach = window_radius[:, 0], window_radius[:, 1]
    kind = jnp.where(row_reach > 0, 1 - time_reach, 2 + time_reach)
    heads = jnp.arange(HEADS, dtype=jnp.int32)
    order = kind * HEADS + heads
    rank = jnp.sum((order[None, :] < order[:, None]).astype(jnp.int32), axis=1)
    perm = jnp.sum(jnp.where(rank[None, :] == heads[:, None], heads[None, :], 0), axis=1)
    reach = jnp.sum(
        jnp.where(rank[None, None, :] == heads[None, :, None], window_radius.T[:, None, :], 0), axis=2
    )
    place = (rank % 2) * SLOTS + rank // 2
    operands = (
        perm, place, reach, frames_valid, rows_valid,
        flat(queries), flat(keys), flat(values), flat(grad_out),
    )
    both = jnp.sum(time_reach * row_reach)
    row_only = jnp.sum(row_reach) - both
    time_only = jnp.sum(time_reach) - both
    choice = jnp.int32(len(PLANS) - 1)
    for index in reversed(range(len(PLANS) - 1)):
        full, high = PLANS[index]
        fits = (
            (both <= 2 * full) & (both + row_only <= 2 * high) & (time_only <= 2 * (SLOTS - high))
        )
        choice = jnp.where(fits, index, choice)
    branches = [
        functools.partial(tile_call, full, high, dims, index)
        for index, (full, high) in enumerate(PLANS)
    ]
    outs = lax.switch(choice, branches, operands) if len(branches) > 1 else branches[0](operands)
    return tuple(unflat(out) for out in outs)


def solution(mesh):
    placed = P("tm", "height", None, None)
    return jax.shard_map(
        on_device,
        mesh=mesh,
        in_specs=(placed, placed, placed, placed, P(), P("tm"), P("height")),
        out_specs=(placed, placed, placed),
        check_vma=False,
    )
```

```python
import functools

import jax
import jax.numpy as jnp
from jax import lax
from jax.experimental import pallas as pl
from jax.experimental.pallas import tpu as pltpu
from jax.sharding import PartitionSpec as P

HEADS = 12
HD = 128
SLOTS = HEADS // 2
PLANS = ((1, 3), (2, 3), (2, 4), (3, 4), (3, 5), (4, 5), (SLOTS, SLOTS))
MESH = pl.DeviceIdType.MESH
F32 = jnp.float32
BF16 = jnp.bfloat16
LOG2E = 1.4426950408889634
MASKED = -1e30


def contract(lhs, rhs, lhs_dim, rhs_dim):
    return lax.dot_general(
        lhs, rhs, (((lhs_dim,), (rhs_dim,)), ((), ())), preferred_element_type=F32
    )


def key_bias(frame_counts, row_counts, time_reach, row_reach, n_time, n_row, frames, rows, tokens):
    count = n_time * n_row * tokens
    lane = lax.broadcasted_iota(jnp.int32, (1, count), 1)

    def steps(position, step, limit):
        total = jnp.zeros_like(position)
        for k in range(1, limit):
            total = total + jnp.where(position >= k * step, 1, 0)
        return total

    time_tile = steps(lane, n_row * tokens, n_time)
    in_time = lane - time_tile * (n_row * tokens)
    row_tile = steps(in_time, tokens, n_row)
    token = in_time - row_tile * tokens
    frame = steps(token, tokens // frames, frames)
    row = lane & (rows - 1)

    def picked(tile, counts, reach):
        if len(counts) == 1:
            return counts[0]
        outer = jnp.where(reach > 0, 1, 0)
        return jnp.where(
            tile == 1, counts[1], jnp.where(tile == 0, counts[0], counts[2]) * outer
        )

    inside = (frame < picked(time_tile, frame_counts, time_reach)) & (
        row < picked(row_tile, row_counts, row_reach)
    )
    return jnp.where(inside, 0.0, MASKED).astype(F32)


def attend(query, key, value, grad, bias):
    scale = HD**-0.5
    scores = contract(query, key, 1, 1) + bias
    row_max = jnp.max(scores, axis=1, keepdims=True)
    raised = jnp.exp2((scores - row_max) * (scale * LOG2E))
    weights = raised * (1.0 / jnp.sum(raised, axis=1, keepdims=True))
    weights_low = weights.astype(BF16)
    output = contract(weights_low, value, 1, 0).astype(BF16).astype(F32)
    row_delta = jnp.sum(output * grad.astype(F32), axis=1, keepdims=True)
    grad_weights = contract(grad, value, 1, 1)
    grad_low = (weights * (grad_weights - row_delta)).astype(BF16)
    grad_query = contract(grad_low, key, 1, 0) * scale
    grad_key = contract(grad_low, query, 0, 0) * scale
    grad_value = contract(weights_low, grad, 0, 0)
    return grad_query, grad_key, grad_value


def kernel(
    full, high, dims,
    perm, place, radius, fv, rv, q_in, k_in, v_in, g_in, dq_out, dk_out, dv_out,
    qg, kv, part, ret_y, ret_z, z_out, sums, result, stage, heads, frame_counts, row_counts,
    swap_s, swap_r, z_s, z_r, y_s, y_r, ry_s, ry_r, rz_s, rz_r, back_s, back_r,
    n_s, n_r,
):
    frames, rows, tokens, n_tm, n_height = dims
    tm = lax.axis_index("tm")
    height = lax.axis_index("height")
    chip = tm // 2
    core = tm % 2
    other = 1 - core
    sibling = (chip * 2 + other, height)
    z_next = ((tm + 2) % n_tm, height)
    z_prev = ((tm + n_tm - 2) % n_tm, height)
    y_next = (tm, (height + 1) % n_height)
    y_prev = (tm, (height + n_height - 1) % n_height)
    z_dev = (z_next, z_prev)
    y_dev = (y_next, y_prev)
    half = n_height // 2
    relay = (height == n_height - 1, height == 0)
    entry = (height == half - 1, height == half)
    far = (
        (tm, jnp.where(entry[0], n_height - 1, jnp.where(relay[0], half, height + 1))),
        (tm, jnp.where(entry[1], 0, jnp.where(relay[1], half - 1, height - 1))),
    )
    land = (jnp.where(entry[0], 1, 0), jnp.where(entry[1], 0, 1))
    origin = (jnp.where(relay[0], 2, 1), jnp.where(relay[1], 0, 1))
    special = relay[0] | relay[1] | entry[0] | entry[1]
    upper = height >= half
    at_end = relay[0] | relay[1]
    greet_first = jnp.where(at_end, jnp.where(upper, half - 1, half), jnp.where(upper, 0, n_height - 1))
    greet_second = jnp.where(at_end, jnp.where(upper, half, half - 1), jnp.where(upper, n_height - 1, 0))

    def remote(src, dst, send, recv, device):
        return pltpu.make_async_remote_copy(
            src_ref=src, dst_ref=dst, send_sem=send, recv_sem=recv,
            device_id=device, device_id_type=MESH,
        )

    barrier = pltpu.get_barrier_semaphore()
    for device in (sibling, z_next, z_prev, y_next, y_prev):
        pl.semaphore_signal(barrier, inc=1, device_id=device, device_id_type=MESH)

    @pl.when(special)
    def _():
        for device in ((tm, greet_first), (tm, greet_second)):
            pl.semaphore_signal(barrier, inc=1, device_id=device, device_id_type=MESH)

    frame_counts[1 + core] = jnp.full((8, 128), fv[0], jnp.int32)
    row_counts[1] = jnp.full((8, 128), rv[0], jnp.int32)

    for head in range(HEADS):
        lanes = pl.ds(head * HD, HD)
        for index, source in enumerate((k_in, v_in, q_in, g_in)):
            heads[head, index] = source[:, lanes]

    def pack(slot, _):
        theirs = perm[2 * slot + other]
        mine = perm[2 * slot + core]
        stage[slot] = heads[theirs]
        block = heads[mine]
        kv[slot, 0, 1 + core, 1] = block[0]
        kv[slot, 1, 1 + core, 1] = block[1]
        qg[slot, 0, core] = block[2]
        qg[slot, 1, core] = block[3]
        return 0

    lax.fori_loop(0, SLOTS, pack, 0)

    for way in range(2):
        @pl.when(relay[way])
        def _(way=way):
            def clear(slot, _):
                kv[slot, 0, :, 2 * (1 - way)] = jnp.zeros((4, tokens, HD), BF16)
                return 0

            lax.fori_loop(0, SLOTS, clear, 0)

    @pl.when(special)
    def _():
        pl.semaphore_wait(barrier, 7)

    @pl.when(jnp.logical_not(special))
    def _():
        pl.semaphore_wait(barrier, 5)

    def counts_swap():
        return remote(
            frame_counts.at[1 + core], frame_counts.at[1 + core], n_s.at[0], n_r.at[0], sibling
        )

    def counts_z(way):
        return remote(
            frame_counts.at[2 - way], frame_counts.at[3 * way], n_s.at[1 + way], n_r.at[1 + way],
            z_dev[way],
        )

    def counts_y(way):
        return remote(
            row_counts.at[1], row_counts.at[2 * way], n_s.at[3 + way], n_r.at[3 + way], y_dev[way]
        )

    def swap_kv(slot):
        return remote(
            stage.at[slot, pl.ds(0, 2)], kv.at[slot, :, 1 + core, 1], swap_s.at[0, slot],
            swap_r.at[0, slot], sibling,
        )

    def swap_qg(slot):
        return remote(
            stage.at[slot, pl.ds(2, 2)], qg.at[slot, :, core], swap_s.at[1, slot],
            swap_r.at[1, slot], sibling,
        )

    def send_z(slot, way):
        return remote(
            kv.at[slot, :, 2 - way, 1], kv.at[slot, :, 3 * way, 1], z_s.at[way, slot],
            z_r.at[way, slot], z_dev[way],
        )

    times = (pl.ds(1, 2), pl.ds(0, 1), pl.ds(3, 1))

    def send_y(slot, way, kind, group):
        time = times[group]
        start, stop, device = (1, way, y_dev[way]) if kind == 0 else (origin[way], land[way], far[way])
        return remote(
            kv.at[slot, kind, time, start], kv.at[slot, kind, time, 2 * stop],
            y_s.at[group, kind, way, slot], y_r.at[group, kind, stop, slot], device,
        )

    def arrive_y(slot, way, kind, group):
        time = times[group]
        return remote(
            kv.at[slot, kind, time, 1], kv.at[slot, kind, time, 2 * way],
            y_s.at[group, kind, way, slot], y_r.at[group, kind, way, slot], y_dev[way],
        )

    def start_y(slot, group):
        for way in range(2):
            @pl.when(jnp.logical_not(relay[way]))
            def _(way=way):
                send_y(slot, way, 0, group).start()
                send_y(slot, way, 1, group).start()

        for way in range(2):
            @pl.when(relay[way])
            def _(way=way):
                arrive_y(slot, 1 - way, 1, group).wait_recv()
                send_y(slot, way, 1, group).start()

    def wait_y(slot, groups):
        for way in range(2):
            @pl.when(jnp.logical_not(relay[1 - way]))
            def _(way=way):
                for group in groups:
                    for kind in range(2):
                        arrive_y(slot, way, kind, group).wait_recv()

    def return_y(slot, way, kind, time):
        stop, device = (way, y_dev[way]) if kind == 0 else (land[way], far[way])
        return remote(
            part.at[slot, kind, time, 2 * (1 - way)], ret_y.at[stop, slot, kind, time],
            ry_s.at[kind, way, slot], ry_r.at[kind, stop, slot], device,
        )

    def returned_y(slot, way, kind, time):
        return remote(
            part.at[slot, kind, time, 2 * (1 - way)], ret_y.at[way, slot, kind, time],
            ry_s.at[kind, way, slot], ry_r.at[kind, way, slot], y_dev[way],
        )

    def relay_y(slot, way, time):
        return remote(
            ret_y.at[1 - way, slot, 1, time], ret_y.at[way, slot, 1, time],
            ry_s.at[1, way, slot], ry_r.at[1, way, slot], far[way],
        )

    def start_return(slot, time):
        for way in range(2):
            @pl.when(jnp.logical_not(relay[way]))
            def _(way=way):
                for kind in range(2):
                    return_y(slot, way, kind, time).start()

    def pass_return(slot, time):
        for way in range(2):
            @pl.when(relay[way])
            def _(way=way):
                returned_y(slot, 1 - way, 1, time).wait_recv()
                relay_y(slot, way, time).start()

    def wait_return(slot, time):
        for way in range(2):
            @pl.when(jnp.logical_not(relay[1 - way]))
            def _(way=way):
                for kind in range(2):
                    returned_y(slot, way, kind, time).wait_recv()

    def return_z(slot, way):
        return remote(
            z_out.at[way, slot], ret_z.at[way, slot], rz_s.at[way, slot], rz_r.at[way, slot],
            z_dev[way],
        )

    def send_back(slot):
        return remote(
            result.at[2 * SLOTS + slot], result.at[core * SLOTS + slot], back_s.at[slot],
            back_r.at[slot], sibling,
        )

    counts_swap().start()
    for way in range(2):
        counts_y(way).start()

    def loop(start, stop, body):
        if stop > start:
            def step(slot, _):
                body(slot)
                return 0
            lax.fori_loop(start, stop, step, 0)

    loop(0, SLOTS, lambda slot: swap_kv(slot).start())
    loop(0, SLOTS, lambda slot: swap_qg(slot).start())
    counts_swap().wait_recv()
    for way in range(2):
        counts_z(way).start()

    def first_z(slot):
        swap_kv(slot).wait_recv()
        for way in range(2):
            send_z(slot, way).start()

    loop(0, full, first_z)
    loop(full, high, lambda slot: swap_kv(slot).wait_recv())
    loop(high, SLOTS, first_z)
    if full:
        start_y(0, 0)

    def corners(slot):
        @pl.when(slot + 1 < full)
        def _():
            start_y(slot + 1, 0)

        for side in range(2):
            send_z(slot, side).wait_recv()
            start_y(slot, 1 + side)

    loop(0, full, corners)
    loop(full, high, lambda slot: start_y(slot, 0))

    for way in range(2):
        counts_z(way).wait_recv()
        counts_y(way).wait_recv()

    edges_time = (
        jnp.where(chip > 0, 1, 0), 1, 1, jnp.where(chip < n_tm // 2 - 1, 1, 0)
    )
    edges_row = (
        jnp.where(height > 0, 1, 0), 1, jnp.where(height < n_height - 1, 1, 0)
    )

    def frame_count(time):
        return frame_counts[time, 0:1, 0:1] * edges_time[time]

    def row_count(row):
        return row_counts[row, 0:1, 0:1] * edges_row[row]

    def compute(slot, n_time, n_row):
        time_reach, row_reach = radius[0, 2 * slot + core], radius[1, 2 * slot + core]
        swap_qg(slot).wait_recv()
        first_row = 0 if n_row == 3 else 1
        key_parts = []
        value_parts = []
        for tile in range(2):
            first_time = tile if n_time == 3 else tile + 1
            bias = key_bias(
                [frame_count(first_time + k) for k in range(n_time)],
                [row_count(first_row + k) for k in range(n_row)],
                time_reach, row_reach, n_time, n_row, frames, rows, tokens,
            )
            span = (pl.ds(first_time, n_time), pl.ds(first_row, n_row))
            count = n_time * n_row * tokens
            key = kv[slot, 0, span[0], span[1]].reshape(count, HD)
            value = kv[slot, 1, span[0], span[1]].reshape(count, HD)
            grad_query, grad_key, grad_value = attend(
                qg[slot, 0, tile], key, value, qg[slot, 1, tile], bias
            )
            low = grad_query.astype(BF16)

            @pl.when(core == tile)
            def _(low=low):
                result[core * SLOTS + slot, 0] = low

            @pl.when(core != tile)
            def _(low=low):
                result[2 * SLOTS + slot, 0] = low

            key_parts.append(grad_key)
            value_parts.append(grad_value)
        where = pl.ds(first_row, n_row)
        width = n_row * tokens

        def put(kind, time, total):
            part[slot, kind, time, where] = total.astype(BF16).reshape(n_row, tokens, HD)

        for kind, parts in ((0, key_parts), (1, value_parts)):
            if n_time == 3:
                put(kind, 0, parts[0][:width])
                for time in (1, 2):
                    put(
                        kind, time,
                        parts[0][time * width : (time + 1) * width]
                        + parts[1][(time - 1) * width : time * width],
                    )
                put(kind, 3, parts[1][2 * width :])
            else:
                put(kind, 1, parts[0])
                put(kind, 2, parts[1])

    every = pl.ds(0, 4)
    own = pl.ds(1, 2)

    def compute_full(slot):
        wait_y(slot, (0, 1, 2))
        compute(slot, 3, 3)
        start_return(slot, every)

        @pl.when(slot > 0)
        def _():
            pass_return(slot - 1, every)

    def compute_high(slot):
        wait_y(slot, (0,))
        compute(slot, 1, 3)
        start_return(slot, own)

        @pl.when(slot > full)
        def _():
            pass_return(slot - 1, own)

    def compute_wide(slot):
        for way in range(2):
            send_z(slot, way).wait_recv()
        compute(slot, 3, 1)
        for kind in range(2):
            for time in (1, 2):
                sums[slot, kind, time - 1] = part[slot, kind, time, 1].astype(F32)
            z_out[0, slot, kind] = part[slot, kind, 3, 1]
            z_out[1, slot, kind] = part[slot, kind, 0, 1]
        for way in range(2):
            return_z(slot, way).start()

    def reduced(slot, kind, time):
        total = part[slot, kind, time, 1].astype(F32)
        for way in range(2):
            block = ret_y[way, slot, kind, time].astype(F32)
            total = total + jnp.where(relay[1 - way], 0.0, block)
        return total

    def reduce_full(slot):
        wait_return(slot, every)
        for kind in range(2):
            for time in (1, 2):
                sums[slot, kind, time - 1] = reduced(slot, kind, time)
            z_out[0, slot, kind] = reduced(slot, kind, 3).astype(BF16)
            z_out[1, slot, kind] = reduced(slot, kind, 0).astype(BF16)
        for way in range(2):
            return_z(slot, way).start()

    def reduce_high(slot):
        wait_return(slot, own)
        for kind in range(2):
            for time in (1, 2):
                sums[slot, kind, time - 1] = reduced(slot, kind, time)

    def step_full(slot):
        compute_full(slot)

        @pl.when(slot > 1)
        def _():
            reduce_full(slot - 2)

    loop(0, full, step_full)
    if full:
        pass_return(full - 1, every)
    loop(full, high, compute_high)
    loop(high, SLOTS, compute_wide)
    if high > full:
        pass_return(high - 1, own)
    loop(max(full - 2, 0), full, reduce_full)
    loop(full, high, reduce_high)

    def finish(slot, with_z):
        if with_z:
            for way in range(2):
                return_z(slot, way).wait_recv()
        for kind in range(2):
            for tile in range(2):
                total = sums[slot, kind, tile]
                if with_z:
                    total = total + ret_z[tile, slot, kind].astype(F32)
                low = total.astype(BF16)

                @pl.when(core == tile)
                def _(low=low, kind=kind):
                    result[core * SLOTS + slot, 1 + kind] = low

                @pl.when(core != tile)
                def _(low=low, kind=kind):
                    result[2 * SLOTS + slot, 1 + kind] = low

        send_back(slot).start()

    loop(high, SLOTS, lambda slot: finish(slot, True))
    loop(0, full, lambda slot: finish(slot, True))
    loop(full, high, lambda slot: finish(slot, False))

    def drain(slot):
        swap_kv(slot).wait_send()
        swap_qg(slot).wait_send()
        send_back(slot).wait_send()

    def drain_z(slot):
        for way in range(2):
            send_z(slot, way).wait_send()
            return_z(slot, way).wait_send()

    def drain_y(slot, groups, time):
        for way in range(2):
            @pl.when(jnp.logical_not(relay[way]))
            def _(way=way):
                for group in groups:
                    send_y(slot, way, 0, group).wait_send()
                return_y(slot, way, 0, time).wait_send()

            for group in groups:
                send_y(slot, way, 1, group).wait_send()
            return_y(slot, way, 1, time).wait_send()

    loop(0, SLOTS, drain)
    loop(0, full, drain_z)
    loop(high, SLOTS, drain_z)
    loop(0, full, lambda slot: drain_y(slot, (0, 1, 2), every))
    loop(full, high, lambda slot: drain_y(slot, (0,), own))
    counts_swap().wait_send()
    for way in range(2):
        counts_z(way).wait_send()
        counts_y(way).wait_send()

    loop(0, SLOTS, lambda slot: send_back(slot).wait_recv())

    for head in range(HEADS):
        lanes = pl.ds(head * HD, HD)
        where = place[head]
        block = result[where]
        dq_out[:, lanes] = block[0]
        dk_out[:, lanes] = block[1]
        dv_out[:, lanes] = block[2]


def tile_call(full, high, dims, collective_id, operands):
    frames, rows, tokens, n_tm, n_height = dims
    width = HEADS * HD
    smem = pl.BlockSpec(memory_space=pltpu.SMEM)
    vmem = pl.BlockSpec(memory_space=pltpu.VMEM)
    dma = pltpu.SemaphoreType.DMA
    tile = (tokens, HD)
    out = jax.ShapeDtypeStruct((tokens, width), BF16)
    return pl.pallas_call(
        functools.partial(kernel, full, high, dims),
        out_shape=(out, out, out),
        in_specs=[smem] * 5 + [vmem] * 4,
        out_specs=(vmem, vmem, vmem),
        scratch_shapes=[
            pltpu.VMEM((SLOTS, 2, 2) + tile, BF16),
            pltpu.VMEM((SLOTS, 2, 4, 3) + tile, BF16),
            pltpu.VMEM((SLOTS, 2, 4, 3) + tile, BF16),
            pltpu.VMEM((2, SLOTS, 2, 4) + tile, BF16),
            pltpu.VMEM((2, SLOTS, 2) + tile, BF16),
            pltpu.VMEM((2, SLOTS, 2) + tile, BF16),
            pltpu.VMEM((SLOTS, 2, 2) + tile, F32),
            pltpu.VMEM((3 * SLOTS, 3) + tile, BF16),
            pltpu.VMEM((SLOTS, 4) + tile, BF16),
            pltpu.VMEM((HEADS, 4) + tile, BF16),
            pltpu.VMEM((4, 8, 128), jnp.int32),
            pltpu.VMEM((3, 8, 128), jnp.int32),
            dma((2, SLOTS)), dma((2, SLOTS)),
            dma((2, SLOTS)), dma((2, SLOTS)),
            dma((3, 2, 2, SLOTS)), dma((3, 2, 2, SLOTS)),
            dma((2, 2, SLOTS)), dma((2, 2, SLOTS)),
            dma((2, SLOTS)), dma((2, SLOTS)),
            dma((SLOTS,)), dma((SLOTS,)),
            dma((5,)), dma((5,)),
        ],
        compiler_params=pltpu.CompilerParams(
            collective_id=collective_id, has_side_effects=True, vmem_limit_bytes=56 << 20
        ),
        cost_estimate=pl.CostEstimate(
            flops=2 * 6 * tokens * 9 * tokens * width, bytes_accessed=7 * 2 * tokens * width,
            transcendentals=9 * tokens * tokens * HEADS,
        ),
    )(*operands)


def on_device(queries, keys, values, grad_out, window_radius, frames_valid, rows_valid):
    frames, rows, columns, width = queries.shape
    tokens = frames * rows * columns

    def flat(block):
        return block.transpose(0, 2, 1, 3).reshape(tokens, width)

    def unflat(block):
        return block.reshape(frames, columns, rows, width).transpose(0, 2, 1, 3)

    dims = (frames, rows, tokens, lax.axis_size("tm"), lax.axis_size("height"))
    time_reach, row_reach = window_radius[:, 0], window_radius[:, 1]
    kind = jnp.where(row_reach > 0, 1 - time_reach, 2 + time_reach)
    heads = jnp.arange(HEADS, dtype=jnp.int32)
    order = kind * HEADS + heads
    rank = jnp.sum((order[None, :] < order[:, None]).astype(jnp.int32), axis=1)
    perm = jnp.sum(jnp.where(rank[None, :] == heads[:, None], heads[None, :], 0), axis=1)
    reach = jnp.sum(
        jnp.where(rank[None, None, :] == heads[None, :, None], window_radius.T[:, None, :], 0), axis=2
    )
    place = (rank % 2) * SLOTS + rank // 2
    operands = (
        perm, place, reach, frames_valid, rows_valid,
        flat(queries), flat(keys), flat(values), flat(grad_out),
    )
    both = jnp.sum(time_reach * row_reach)
    row_only = jnp.sum(row_reach) - both
    time_only = jnp.sum(time_reach) - both
    fulls, highs = jnp.asarray(PLANS, jnp.int32).T
    fits = (
        (both <= 2 * fulls) & (both + row_only <= 2 * highs) & (time_only <= 2 * (SLOTS - highs))
    )
    index = jnp.arange(len(PLANS), dtype=jnp.int32)
    choice = jnp.min(jnp.where(fits, index, len(PLANS) - 1))
    branches = [
        functools.partial(tile_call, full, high, dims, index)
        for index, (full, high) in enumerate(PLANS)
    ]
    outs = lax.switch(choice, branches, operands) if len(branches) > 1 else branches[0](operands)
    return tuple(unflat(out) for out in outs)


def solution(mesh):
    placed = P("tm", "height", None, None)
    return jax.shard_map(
        on_device,
        mesh=mesh,
        in_specs=(placed, placed, placed, placed, P(), P("tm"), P("height")),
        out_specs=(placed, placed, placed),
        check_vma=False,
    )
```

```python
import functools

import jax
import jax.numpy as jnp
from jax import lax
from jax.experimental import pallas as pl
from jax.experimental.pallas import tpu as pltpu
from jax.sharding import PartitionSpec as P

HEADS = 12
HD = 128
SLOTS = HEADS // 2
PLANS = ((1, 3), (2, 3), (2, 4), (3, 4), (3, 5), (4, 5), (SLOTS, SLOTS))
MESH = pl.DeviceIdType.MESH
F32 = jnp.float32
BF16 = jnp.bfloat16
LOG2E = 1.4426950408889634
MASKED = -1e30


def contract(lhs, rhs, lhs_dim, rhs_dim):
    return lax.dot_general(
        lhs, rhs, (((lhs_dim,), (rhs_dim,)), ((), ())), preferred_element_type=F32
    )


def key_bias(frame_counts, row_counts, time_reach, row_reach, n_time, n_row, frames, rows, tokens):
    count = n_time * n_row * tokens
    lane = lax.broadcasted_iota(jnp.int32, (1, count), 1)

    def steps(position, step, limit):
        total = jnp.zeros_like(position)
        for k in range(1, limit):
            total = total + jnp.where(position >= k * step, 1, 0)
        return total

    time_tile = steps(lane, n_row * tokens, n_time)
    in_time = lane - time_tile * (n_row * tokens)
    row_tile = steps(in_time, tokens, n_row)
    token = in_time - row_tile * tokens
    frame = steps(token, tokens // frames, frames)
    row = lane & (rows - 1)

    def picked(tile, counts, reach):
        if len(counts) == 1:
            return counts[0]
        outer = jnp.where(reach > 0, 1, 0)
        return jnp.where(
            tile == 1, counts[1], jnp.where(tile == 0, counts[0], counts[2]) * outer
        )

    inside = (frame < picked(time_tile, frame_counts, time_reach)) & (
        row < picked(row_tile, row_counts, row_reach)
    )
    return jnp.where(inside, 0.0, MASKED).astype(F32)


def attend(query, key, value, grad, bias):
    scale = HD**-0.5
    scores = contract(query, key, 1, 1) + bias
    row_max = jnp.max(scores, axis=1, keepdims=True)
    raised = jnp.exp2((scores - row_max) * (scale * LOG2E))
    weights = raised * (1.0 / jnp.sum(raised, axis=1, keepdims=True))
    weights_low = weights.astype(BF16)
    output = contract(weights_low, value, 1, 0).astype(BF16).astype(F32)
    row_delta = jnp.sum(output * grad.astype(F32), axis=1, keepdims=True)
    grad_weights = contract(grad, value, 1, 1)
    grad_low = (weights * (grad_weights - row_delta)).astype(BF16)
    grad_query = contract(grad_low, key, 1, 0) * scale
    grad_key = contract(grad_low, query, 0, 0) * scale
    grad_value = contract(weights_low, grad, 0, 0)
    return grad_query, grad_key, grad_value


def kernel(
    full, high, dims,
    perm, place, radius, fv, rv, q_in, k_in, v_in, g_in, dq_out, dk_out, dv_out,
    qg, kv, part, ret_y, ret_z, z_out, sums, total, result, stage, heads, frame_counts, row_counts,
    swap_s, swap_r, z_s, z_r, y_s, y_r, ry_s, ry_r, rz_s, rz_r, back_s, back_r,
    n_s, n_r,
):
    frames, rows, tokens, n_tm, n_height = dims
    tm = lax.axis_index("tm")
    height = lax.axis_index("height")
    chip = tm // 2
    core = tm % 2
    other = 1 - core
    sibling = (chip * 2 + other, height)
    z_next = ((tm + 2) % n_tm, height)
    z_prev = ((tm + n_tm - 2) % n_tm, height)
    y_next = (tm, (height + 1) % n_height)
    y_prev = (tm, (height + n_height - 1) % n_height)
    z_dev = (z_next, z_prev)
    y_dev = (y_next, y_prev)
    half = n_height // 2
    relay = (height == n_height - 1, height == 0)
    entry = (height == half - 1, height == half)
    far = (
        (tm, jnp.where(entry[0], n_height - 1, jnp.where(relay[0], half, height + 1))),
        (tm, jnp.where(entry[1], 0, jnp.where(relay[1], half - 1, height - 1))),
    )
    land = (jnp.where(entry[0], 1, 0), jnp.where(entry[1], 0, 1))
    origin = (jnp.where(relay[0], 2, 1), jnp.where(relay[1], 0, 1))
    special = relay[0] | relay[1] | entry[0] | entry[1]
    upper = height >= half
    at_end = relay[0] | relay[1]
    greet_first = jnp.where(at_end, jnp.where(upper, half - 1, half), jnp.where(upper, 0, n_height - 1))
    greet_second = jnp.where(at_end, jnp.where(upper, half, half - 1), jnp.where(upper, n_height - 1, 0))

    def remote(src, dst, send, recv, device):
        return pltpu.make_async_remote_copy(
            src_ref=src, dst_ref=dst, send_sem=send, recv_sem=recv,
            device_id=device, device_id_type=MESH,
        )

    barrier = pltpu.get_barrier_semaphore()
    for device in (sibling, z_next, z_prev, y_next, y_prev):
        pl.semaphore_signal(barrier, inc=1, device_id=device, device_id_type=MESH)

    @pl.when(special)
    def _():
        for device in ((tm, greet_first), (tm, greet_second)):
            pl.semaphore_signal(barrier, inc=1, device_id=device, device_id_type=MESH)

    frame_counts[1 + core] = jnp.full((8, 128), fv[0], jnp.int32)
    row_counts[1] = jnp.full((8, 128), rv[0], jnp.int32)

    for head in range(HEADS):
        lanes = pl.ds(head * HD, HD)
        for index, source in enumerate((k_in, v_in, q_in, g_in)):
            heads[head, index] = source[:, lanes]

    def pack(slot, _):
        theirs = perm[2 * slot + other]
        mine = perm[2 * slot + core]
        stage[slot] = heads[theirs]
        block = heads[mine]
        kv[slot, 0, 1 + core, 1] = block[0]
        kv[slot, 1, 1 + core, 1] = block[1]
        qg[slot, 0, core] = block[2]
        qg[slot, 1, core] = block[3]
        return 0

    lax.fori_loop(0, SLOTS, pack, 0)

    for way in range(2):
        @pl.when(relay[way])
        def _(way=way):
            def clear(slot, _):
                kv[slot, 0, :, 2 * (1 - way)] = jnp.zeros((4, tokens, HD), BF16)
                return 0

            lax.fori_loop(0, SLOTS, clear, 0)

    @pl.when(special)
    def _():
        pl.semaphore_wait(barrier, 7)

    @pl.when(jnp.logical_not(special))
    def _():
        pl.semaphore_wait(barrier, 5)

    def counts_swap():
        return remote(
            frame_counts.at[1 + core], frame_counts.at[1 + core], n_s.at[0], n_r.at[0], sibling
        )

    def counts_z(way):
        return remote(
            frame_counts.at[2 - way], frame_counts.at[3 * way], n_s.at[1 + way], n_r.at[1 + way],
            z_dev[way],
        )

    def counts_y(way):
        return remote(
            row_counts.at[1], row_counts.at[2 * way], n_s.at[3 + way], n_r.at[3 + way], y_dev[way]
        )

    def swap_kv(slot):
        return remote(
            stage.at[slot, pl.ds(0, 2)], kv.at[slot, :, 1 + core, 1], swap_s.at[0, slot],
            swap_r.at[0, slot], sibling,
        )

    def swap_qg(slot):
        return remote(
            stage.at[slot, pl.ds(2, 2)], qg.at[slot, :, core], swap_s.at[1, slot],
            swap_r.at[1, slot], sibling,
        )

    def send_z(slot, way):
        return remote(
            kv.at[slot, :, 2 - way, 1], kv.at[slot, :, 3 * way, 1], z_s.at[way, slot],
            z_r.at[way, slot], z_dev[way],
        )

    times = (pl.ds(1, 2), pl.ds(0, 1), pl.ds(3, 1))

    def send_y(slot, way, kind, group):
        time = times[group]
        start, stop, device = (1, way, y_dev[way]) if kind == 0 else (origin[way], land[way], far[way])
        return remote(
            kv.at[slot, kind, time, start], kv.at[slot, kind, time, 2 * stop],
            y_s.at[group, kind, way, slot], y_r.at[group, kind, stop, slot], device,
        )

    def arrive_y(slot, way, kind, group):
        time = times[group]
        return remote(
            kv.at[slot, kind, time, 1], kv.at[slot, kind, time, 2 * way],
            y_s.at[group, kind, way, slot], y_r.at[group, kind, way, slot], y_dev[way],
        )

    def start_y(slot, group):
        for way in range(2):
            @pl.when(jnp.logical_not(relay[way]))
            def _(way=way):
                send_y(slot, way, 0, group).start()
                send_y(slot, way, 1, group).start()

        for way in range(2):
            @pl.when(relay[way])
            def _(way=way):
                arrive_y(slot, 1 - way, 1, group).wait_recv()
                send_y(slot, way, 1, group).start()

    def wait_y(slot, groups):
        for way in range(2):
            @pl.when(jnp.logical_not(relay[1 - way]))
            def _(way=way):
                for group in groups:
                    for kind in range(2):
                        arrive_y(slot, way, kind, group).wait_recv()

    def return_y(slot, way, kind, time):
        stop, device = (way, y_dev[way]) if kind == 0 else (land[way], far[way])
        return remote(
            part.at[slot, kind, time, 2 * (1 - way)], ret_y.at[stop, slot, kind, time],
            ry_s.at[kind, way, slot], ry_r.at[kind, stop, slot], device,
        )

    def returned_y(slot, way, kind, time):
        return remote(
            part.at[slot, kind, time, 2 * (1 - way)], ret_y.at[way, slot, kind, time],
            ry_s.at[kind, way, slot], ry_r.at[kind, way, slot], y_dev[way],
        )

    def relay_y(slot, way, time):
        return remote(
            ret_y.at[1 - way, slot, 1, time], ret_y.at[way, slot, 1, time],
            ry_s.at[1, way, slot], ry_r.at[1, way, slot], far[way],
        )

    def start_return(slot, time):
        for way in range(2):
            @pl.when(jnp.logical_not(relay[way]))
            def _(way=way):
                for kind in range(2):
                    return_y(slot, way, kind, time).start()

    def pass_return(slot, time):
        for way in range(2):
            @pl.when(relay[way])
            def _(way=way):
                returned_y(slot, 1 - way, 1, time).wait_recv()
                relay_y(slot, way, time).start()

    def wait_return(slot, time):
        for way in range(2):
            @pl.when(jnp.logical_not(relay[1 - way]))
            def _(way=way):
                for kind in range(2):
                    returned_y(slot, way, kind, time).wait_recv()

    def return_z(slot, way):
        return remote(
            z_out.at[way, slot], ret_z.at[way, slot], rz_s.at[way, slot], rz_r.at[way, slot],
            z_dev[way],
        )

    def send_back(slot):
        return remote(
            result.at[2 * SLOTS + slot], result.at[core * SLOTS + slot], back_s.at[slot],
            back_r.at[slot], sibling,
        )

    counts_swap().start()
    for way in range(2):
        counts_y(way).start()

    def loop(start, stop, body):
        if stop > start:
            def step(slot, _):
                body(slot)
                return 0
            lax.fori_loop(start, stop, step, 0)

    loop(0, SLOTS, lambda slot: swap_kv(slot).start())
    loop(0, SLOTS, lambda slot: swap_qg(slot).start())
    counts_swap().wait_recv()
    for way in range(2):
        counts_z(way).start()

    def first_z(slot):
        swap_kv(slot).wait_recv()
        for way in range(2):
            send_z(slot, way).start()

    loop(0, full, first_z)
    loop(full, high, lambda slot: swap_kv(slot).wait_recv())
    loop(high, SLOTS, first_z)
    if full:
        start_y(0, 0)

    def corners(slot):
        @pl.when(slot + 1 < full)
        def _():
            start_y(slot + 1, 0)

        for side in range(2):
            send_z(slot, side).wait_recv()
            start_y(slot, 1 + side)

    if full == SLOTS:
        corners(0)
    else:
        loop(0, full, corners)
    loop(full, high, lambda slot: start_y(slot, 0))

    for way in range(2):
        counts_z(way).wait_recv()
        counts_y(way).wait_recv()

    first_edge = jnp.where(chip > 0, 1, 0)
    last_edge = jnp.where(chip < n_tm // 2 - 1, 1, 0)
    edges_row = (
        jnp.where(height > 0, 1, 0), 1, jnp.where(height < n_height - 1, 1, 0)
    )

    def frame_count(time):
        inside = jnp.where(time == 0, first_edge, jnp.where(time == 3, last_edge, 1))
        return frame_counts[time, 0:1, 0:1] * inside

    def row_count(row):
        return row_counts[row, 0:1, 0:1] * edges_row[row]

    def compute(slot, n_time, n_row):
        time_reach, row_reach = radius[0, 2 * slot + core], radius[1, 2 * slot + core]
        swap_qg(slot).wait_recv()
        first_row = 0 if n_row == 3 else 1
        where = pl.ds(first_row, n_row)
        count = n_time * n_row * tokens
        span = (n_time, n_row, tokens, HD)
        if n_time == 3:
            def clear(time, _):
                total[:, time, where] = jnp.zeros((2, n_row, tokens, HD), F32)
                return 0

            lax.fori_loop(0, 4, clear, 0)

        def one_tile(tile, _):
            first_time = tile if n_time == 3 else tile + 1
            bias = key_bias(
                [frame_count(first_time + k) for k in range(n_time)],
                [row_count(first_row + k) for k in range(n_row)],
                time_reach, row_reach, n_time, n_row, frames, rows, tokens,
            )
            key = kv[slot, 0, pl.ds(first_time, n_time), where].reshape(count, HD)
            value = kv[slot, 1, pl.ds(first_time, n_time), where].reshape(count, HD)
            grad_query, grad_key, grad_value = attend(
                qg[slot, 0, tile], key, value, qg[slot, 1, tile], bias
            )
            row = jnp.where(core == tile, core, 2) * SLOTS + slot
            result[row, 0] = grad_query.astype(BF16)
            for kind, block in ((0, grad_key), (1, grad_value)):
                block = block.reshape(span)
                if n_time == 3:
                    total[kind, pl.ds(first_time, n_time), where] += block
                else:
                    part[slot, kind, pl.ds(first_time, n_time), where] = block.astype(BF16)
            return 0

        lax.fori_loop(0, 2, one_tile, 0)
        if n_time == 3:
            def lower(time, _):
                for kind in range(2):
                    part[slot, kind, time, where] = total[kind, time, where].astype(BF16)
                return 0

            lax.fori_loop(0, 4, lower, 0)

    every = pl.ds(0, 4)
    own = pl.ds(1, 2)

    def compute_full(slot):
        wait_y(slot, (0, 1, 2))
        compute(slot, 3, 3)
        start_return(slot, every)

        @pl.when(slot > 0)
        def _():
            pass_return(slot - 1, every)

    def compute_high(slot):
        wait_y(slot, (0,))
        compute(slot, 1, 3)
        start_return(slot, own)

        @pl.when(slot > full)
        def _():
            pass_return(slot - 1, own)

    def compute_wide(slot):
        for way in range(2):
            send_z(slot, way).wait_recv()
        compute(slot, 3, 1)
        for kind in range(2):
            for time in (1, 2):
                sums[slot, kind, time - 1] = part[slot, kind, time, 1].astype(F32)
            z_out[0, slot, kind] = part[slot, kind, 3, 1]
            z_out[1, slot, kind] = part[slot, kind, 0, 1]
        for way in range(2):
            return_z(slot, way).start()

    def reduced(slot, kind, time):
        share = part[slot, kind, time, 1].astype(F32)
        for way in range(2):
            block = ret_y[way, slot, kind, time].astype(F32)
            share = share + jnp.where(relay[1 - way], 0.0, block)
        return share

    def reduce_full(slot):
        wait_return(slot, every)
        for kind in range(2):
            for time in (1, 2):
                sums[slot, kind, time - 1] = reduced(slot, kind, time)
            z_out[0, slot, kind] = reduced(slot, kind, 3).astype(BF16)
            z_out[1, slot, kind] = reduced(slot, kind, 0).astype(BF16)
        for way in range(2):
            return_z(slot, way).start()

    def reduce_high(slot):
        wait_return(slot, own)
        for kind in range(2):
            for time in (1, 2):
                sums[slot, kind, time - 1] = reduced(slot, kind, time)

    def step_full(slot):
        if full == SLOTS:
            @pl.when(slot + 1 < full)
            def _():
                corners(slot + 1)

        compute_full(slot)

        @pl.when(slot > 1)
        def _():
            reduce_full(slot - 2)

    loop(0, full, step_full)
    if full:
        pass_return(full - 1, every)
    loop(full, high, compute_high)
    loop(high, SLOTS, compute_wide)
    if high > full:
        pass_return(high - 1, own)
    loop(max(full - 2, 0), full, reduce_full)
    loop(full, high, reduce_high)

    def finish(slot, with_z):
        if with_z:
            for way in range(2):
                return_z(slot, way).wait_recv()
        for kind in range(2):
            for tile in range(2):
                share = sums[slot, kind, tile]
                if with_z:
                    share = share + ret_z[tile, slot, kind].astype(F32)
                low = share.astype(BF16)

                @pl.when(core == tile)
                def _(low=low, kind=kind):
                    result[core * SLOTS + slot, 1 + kind] = low

                @pl.when(core != tile)
                def _(low=low, kind=kind):
                    result[2 * SLOTS + slot, 1 + kind] = low

        send_back(slot).start()

    loop(high, SLOTS, lambda slot: finish(slot, True))
    loop(0, full, lambda slot: finish(slot, True))
    loop(full, high, lambda slot: finish(slot, False))

    def drain(slot):
        swap_kv(slot).wait_send()
        swap_qg(slot).wait_send()
        send_back(slot).wait_send()

    def drain_z(slot):
        for way in range(2):
            send_z(slot, way).wait_send()
            return_z(slot, way).wait_send()

    def drain_y(slot, groups, time):
        for way in range(2):
            @pl.when(jnp.logical_not(relay[way]))
            def _(way=way):
                for group in groups:
                    send_y(slot, way, 0, group).wait_send()
                return_y(slot, way, 0, time).wait_send()

            for group in groups:
                send_y(slot, way, 1, group).wait_send()
            return_y(slot, way, 1, time).wait_send()

    loop(0, SLOTS, drain)
    loop(0, full, drain_z)
    loop(high, SLOTS, drain_z)
    loop(0, full, lambda slot: drain_y(slot, (0, 1, 2), every))
    loop(full, high, lambda slot: drain_y(slot, (0,), own))
    counts_swap().wait_send()
    for way in range(2):
        counts_z(way).wait_send()
        counts_y(way).wait_send()

    loop(0, SLOTS, lambda slot: send_back(slot).wait_recv())

    for head in range(HEADS):
        lanes = pl.ds(head * HD, HD)
        where = place[head]
        block = result[where]
        dq_out[:, lanes] = block[0]
        dk_out[:, lanes] = block[1]
        dv_out[:, lanes] = block[2]


def tile_call(full, high, dims, collective_id, operands):
    frames, rows, tokens, n_tm, n_height = dims
    width = HEADS * HD
    smem = pl.BlockSpec(memory_space=pltpu.SMEM)
    vmem = pl.BlockSpec(memory_space=pltpu.VMEM)
    dma = pltpu.SemaphoreType.DMA
    tile = (tokens, HD)
    out = jax.ShapeDtypeStruct((tokens, width), BF16)
    return pl.pallas_call(
        functools.partial(kernel, full, high, dims),
        out_shape=(out, out, out),
        in_specs=[smem] * 5 + [vmem] * 4,
        out_specs=(vmem, vmem, vmem),
        scratch_shapes=[
            pltpu.VMEM((SLOTS, 2, 2) + tile, BF16),
            pltpu.VMEM((SLOTS, 2, 4, 3) + tile, BF16),
            pltpu.VMEM((SLOTS, 2, 4, 3) + tile, BF16),
            pltpu.VMEM((2, SLOTS, 2, 4) + tile, BF16),
            pltpu.VMEM((2, SLOTS, 2) + tile, BF16),
            pltpu.VMEM((2, SLOTS, 2) + tile, BF16),
            pltpu.VMEM((SLOTS, 2, 2) + tile, F32),
            pltpu.VMEM((2, 4, 3) + tile, F32),
            pltpu.VMEM((3 * SLOTS, 3) + tile, BF16),
            pltpu.VMEM((SLOTS, 4) + tile, BF16),
            pltpu.VMEM((HEADS, 4) + tile, BF16),
            pltpu.VMEM((4, 8, 128), jnp.int32),
            pltpu.VMEM((3, 8, 128), jnp.int32),
            dma((2, SLOTS)), dma((2, SLOTS)),
            dma((2, SLOTS)), dma((2, SLOTS)),
            dma((3, 2, 2, SLOTS)), dma((3, 2, 2, SLOTS)),
            dma((2, 2, SLOTS)), dma((2, 2, SLOTS)),
            dma((2, SLOTS)), dma((2, SLOTS)),
            dma((SLOTS,)), dma((SLOTS,)),
            dma((5,)), dma((5,)),
        ],
        compiler_params=pltpu.CompilerParams(
            collective_id=collective_id, has_side_effects=True, vmem_limit_bytes=56 << 20
        ),
        cost_estimate=pl.CostEstimate(
            flops=2 * 6 * tokens * 9 * tokens * width, bytes_accessed=7 * 2 * tokens * width,
            transcendentals=9 * tokens * tokens * HEADS,
        ),
    )(*operands)


def plan_kernel(radius, perm, place, reach, choice):
    time_reach = [radius[0, head] for head in range(HEADS)]
    row_reach = [radius[1, head] for head in range(HEADS)]
    both = sum(x * y for x, y in zip(time_reach, row_reach))
    row_only = sum(row_reach) - both
    time_only = sum(time_reach) - both
    picked = jnp.int32(len(PLANS) - 1)
    start_high, start_wide = jnp.int32(2 * PLANS[-1][0]), jnp.int32(2 * PLANS[-1][1])
    for index in reversed(range(len(PLANS) - 1)):
        full, high = PLANS[index]
        spill = jnp.maximum(row_only - 2 * (high - full), 0)
        spill = spill + jnp.maximum(time_only - 2 * (SLOTS - high), 0)
        fits = both + spill <= 2 * full
        picked = jnp.where(fits, index, picked)
        start_high = jnp.where(fits, 2 * full, start_high)
        start_wide = jnp.where(fits, 2 * high, start_wide)
    choice[0] = picked

    next_full, next_high, next_wide = jnp.int32(0), start_high, start_wide

    def seat(head, take, prefers_high, prefers_wide):
        nonlocal next_full, next_high, next_wide
        to_high = prefers_high & (next_high < start_wide)
        to_wide = prefers_wide & (next_wide < HEADS) & jnp.logical_not(to_high)
        where = jnp.where(to_high, next_high, jnp.where(to_wide, next_wide, next_full))

        @pl.when(take)
        def _():
            perm[where] = head
            reach[0, where] = time_reach[head]
            reach[1, where] = row_reach[head]
            place[head] = (where & 1) * SLOTS + (where >> 1)

        high, wide = jnp.where(to_high, 1, 0), jnp.where(to_wide, 1, 0)
        taken = jnp.where(take, 1, 0)
        next_high = next_high + taken * high
        next_wide = next_wide + taken * wide
        next_full = next_full + taken * (1 - high - wide)

    for head in range(HEADS):
        along_time, along_row = time_reach[head] > 0, row_reach[head] > 0
        seat(head, along_time | along_row, jnp.logical_not(along_time), jnp.logical_not(along_row))
    for head in range(HEADS):
        take = time_reach[head] + row_reach[head] == 0
        seat(head, take, take, take)


def plan_call(radius):
    smem = pl.BlockSpec(memory_space=pltpu.SMEM)
    line = jax.ShapeDtypeStruct((HEADS,), jnp.int32)
    return pl.pallas_call(
        plan_kernel,
        out_shape=(
            line, line, jax.ShapeDtypeStruct((2, HEADS), jnp.int32),
            jax.ShapeDtypeStruct((1,), jnp.int32),
        ),
        in_specs=[smem],
        out_specs=(smem, smem, smem, smem),
    )(radius)


def on_device(queries, keys, values, grad_out, window_radius, frames_valid, rows_valid):
    frames, rows, columns, width = queries.shape
    tokens = frames * rows * columns

    def flat(block):
        return block.transpose(0, 2, 1, 3).reshape(tokens, width)

    def unflat(block):
        return block.reshape(frames, columns, rows, width).transpose(0, 2, 1, 3)

    dims = (frames, rows, tokens, lax.axis_size("tm"), lax.axis_size("height"))
    perm, place, reach, choice = plan_call(window_radius.T)
    operands = (
        perm, place, reach, frames_valid, rows_valid,
        flat(queries), flat(keys), flat(values), flat(grad_out),
    )
    branches = [
        functools.partial(tile_call, full, high, dims, index)
        for index, (full, high) in enumerate(PLANS)
    ]
    outs = lax.switch(choice[0], branches, operands) if len(branches) > 1 else branches[0](operands)
    return tuple(unflat(out) for out in outs)


def solution(mesh):
    placed = P("tm", "height", None, None)
    return jax.shard_map(
        on_device,
        mesh=mesh,
        in_specs=(placed, placed, placed, placed, P(), P("tm"), P("height")),
        out_specs=(placed, placed, placed),
        check_vma=False,
    )
```
